128 devices in a mesh: tm: 8 (over y_lo, z), row: 16 (over x, y_hi, core).
Axes of the slice: x: 4, y: 4 (y_hi: 2, y_lo: 2; y = y_hi * 2 + y_lo), z: 4, core: 2. Of those that a mesh axis runs over, the one named last changes fastest.
Arguments:
- features: bfloat16 [32, 64, 64, 512], P('tm', 'row'), may hold values from -200 to 200
- norm_gain: float32 [512], replicated, may hold values from 0.1 to 1.9
- norm_bias: float32 [512], replicated, may hold values from -3 to 3
- latent_kernel: bfloat16 [16, 3, 3, 3, 512], replicated, may hold values from -0.0546875 to 0.0546875
- latent_bias: float32 [16], replicated, may hold values from -3 to 3
- token_mask: int32 [32, 64, 64], P('tm', 'row'), may hold values 0 or 1
- embed_weight: bfloat16 [16, 2048], replicated, may hold values from -1.5 to 1.5
- mask_token: float32 [2048], replicated, may hold values from -5 to 5
- pos_embed: bfloat16 [32, 64, 64, 2048], P('tm', 'row'), may hold values from -3 to 3
- query_weight: bfloat16 [2048, 1024], replicated, may hold values from -0.125 to 0.125
- key_weight: bfloat16 [2048, 1024], replicated, may hold values from -0.125 to 0.125
- value_weight: bfloat16 [2048, 1024], replicated, may hold values from -0.125 to 0.125
- logit_scale: float32 [8], replicated, may hold values from 8 to 32
- pattern: int32 [32, 32, 4], P('tm', 'row'), may hold values from -1 to 1023, as said below
Outputs:
- attended: bfloat16 [32, 64, 64, 1024], P('tm', 'row')
The draws below stay inside these ranges and needn't reach their ends.
Inputs may be any that keep to these rules, and one draw needn't show every extreme that they name: `pattern`: row (t, p) lists key blocks for the query block of frame t and row pair p (block id t * 32 + p): first that block itself, then distinct blocks whose frame differs from t by at most one and whose row pair differs from p by at most one; the rest of the row is -1. On every device the first row pair of its first frame lists 4 blocks.
All inputs are finite; a program needn't handle non-finite values. No bound on the sum of `token_mask` on one device may be relied on, other than what follows from the above.
Results may differ from the reference program's by a relative error of at most 0.0085.
Values may be sent and summed in bfloat16 or wider, within the bound.
A program may use at most 128 MiB of HBM per device.

```python
import math
import jax
import jax.numpy as jnp
from jax import lax

C = 512
LAT = 16
D = 2048
HEADS = 8
HD = 128
GROUPS = 32
MAXKB = 4
FT = 4
FR = 4
NW = 64
NT = 32
NH = 64


def draw_features(key, part):
    streams = jax.random.split(key, 4)
    frame_pos = jnp.arange(NT).astype(jnp.float32) / max(NT - 1, 1)
    rising = (3.0 ** frame_pos)[:, None, None, None]
    row_scale = jnp.exp(jax.random.uniform(streams[0], (NT, NH, 1, 1)) * math.log(3.0))
    noise = jax.random.normal(streams[1], (NT, NH, NW, C))
    channel_scale = jnp.exp(jax.random.uniform(streams[2], (C,)) * math.log(3.0))
    channel_mean = 0.5 * jax.random.normal(streams[3], (C,))
    return jnp.clip(channel_mean + rising * row_scale * channel_scale * noise, -200.0, 200.0).astype(jnp.bfloat16)


def draw_pattern(key, part):
    pair_total = NH // 2
    first_key, second_key = jax.random.split(key)
    frame_ids = jnp.arange(NT)[:, None, None]
    pair_ids = jnp.arange(pair_total)[None, :, None]
    frame_steps = jnp.array([-1, -1, -1, 0, 0, 1, 1, 1], jnp.int32)
    pair_steps = jnp.array([-1, 0, 1, -1, 1, -1, 0, 1], jnp.int32)
    key_frame = frame_ids + frame_steps
    key_pair = pair_ids + pair_steps
    inside = (key_frame >= 0) & (key_frame < NT) & (key_pair >= 0) & (key_pair < pair_total)
    random_rank = jax.random.randint(first_key, (NT, pair_total, 8), 0, 1 << 20) * 8 + jnp.arange(8)
    ranking = jnp.where(inside, random_rank, (1 << 24) + jnp.arange(8))
    ordering = jnp.argsort(ranking, axis=-1)
    neighbour_ids = jnp.take_along_axis(key_frame * pair_total + key_pair, ordering, axis=-1)
    inside_count = jnp.sum(inside.astype(jnp.int32), axis=-1)
    listed_count = jax.random.randint(second_key, (NT, pair_total), 1, MAXKB + 1)
    leading = (frame_ids[..., 0] % FT == 0) & (pair_ids[..., 0] % (FR // 2) == 0)
    listed_count = jnp.where(leading, MAXKB, listed_count)
    listed_count = jnp.minimum(listed_count, 1 + inside_count)
    own_ids = frame_ids[..., 0] * pair_total + pair_ids[..., 0]
    entries = jnp.concatenate([own_ids[..., None], neighbour_ids[..., :MAXKB - 1]], axis=-1)
    live_slot = jnp.arange(MAXKB)[None, None, :] < listed_count[..., None]
    return jnp.where(live_slot, entries, -1).astype(jnp.int32)


def place_ends(result, rng, smallest, high):
    longest = result.shape.index(max(result.shape))
    spots = []
    for shift in (0, 1):
        where = [jax.random.randint(jax.random.fold_in(rng, axis), (), 0, length) for axis, length in enumerate(result.shape)]
        where[longest] = (where[longest] + shift) % result.shape[longest]
        spots.append(tuple(where))
    return result.at[spots[0]].set(smallest).at[spots[1]].set(high)


def level_of(key, shape, pieces, smallest, top_value):
    def one(dim, shards_of):
        draws = jax.random.uniform(jax.random.fold_in(jax.random.fold_in(key, 6), dim), (shards_of,), jnp.float32, smallest / len(pieces), top_value / len(pieces))
        return jnp.repeat(jnp.exp(draws), shape[dim] // shards_of).reshape((-1,) + (1,) * (len(shape) - dim - 1))

    gain = one(*pieces[0])
    for cut in pieces[1:]:
        gain = gain * one(*cut)
    return gain


def scatter_about(own_key, shape, deviation, reach, cuts=(), kind=jnp.bfloat16):
    values = jax.random.normal(own_key, shape, jnp.float32) * deviation
    if len(cuts) > 0:
        values = level_of(own_key, shape, cuts, -0.22, 0.18) * values
    return jnp.clip(values, min=-reach, max=reach).astype(kind)


def setup_inputs(seed: int = 0) -> dict:
    streams_of = jax.random.split(jax.random.key(seed), 15)
    features = draw_features(jax.random.fold_in(streams_of[14], 71), 0)
    norm_gain = jnp.clip(1.0 + 0.18 * jax.random.normal(streams_of[1], (C,), jnp.float32), 0.1, 1.9)
    norm_bias = scatter_about(streams_of[2], (C,), 0.5, 3.0, (), jnp.float32)
    latent_kernel = scatter_about(streams_of[3], (LAT, 3, 3, 3, C), (27 * C) ** -0.5, 0.0546875)
    latent_bias = scatter_about(streams_of[4], (LAT,), 0.5, 3.0, (), jnp.float32)
    token_mask = place_ends((jax.random.randint(streams_of[5], (NT, NH, NW), 0, 4) < 1).astype(jnp.int32), jax.random.fold_in(streams_of[5], 1), 0, 1)
    embed_weight = scatter_about(streams_of[6], (LAT, D), LAT ** -0.5, 1.5)
    mask_token = scatter_about(streams_of[7], (D,), 1.0, 5.0, (), jnp.float32)
    pos_embed = scatter_about(streams_of[8], (NT, NH, NW, D), 0.5, 3.0, ((0, 8), (1, 16)))
    query_weight = scatter_about(streams_of[9], (D, HEADS * HD), D ** -0.5, 0.125)
    key_weight = scatter_about(streams_of[10], (D, HEADS * HD), D ** -0.5, 0.125)
    value_weight = scatter_about(streams_of[11], (D, HEADS * HD), D ** -0.5, 0.125)
    logit_scale = jnp.clip(jnp.exp(jax.random.uniform(streams_of[12], (HEADS,), jnp.float32, math.log(8.0), math.log(32.0))), 8.0, 32.0)
    pattern = draw_pattern(jax.random.fold_in(streams_of[14], 71), 0)
    return {"features": features, "norm_gain": norm_gain, "norm_bias": norm_bias, "latent_kernel": latent_kernel, "latent_bias": latent_bias, "token_mask": token_mask, "embed_weight": embed_weight, "mask_token": mask_token, "pos_embed": pos_embed, "query_weight": query_weight, "key_weight": key_weight, "value_weight": value_weight, "logit_scale": logit_scale, "pattern": pattern}


def unit_heads(values, head_count):
    shaped = values.astype(jnp.float32).reshape(values.shape[0], head_count, -1)
    normal = shaped * lax.rsqrt(lax.optimization_barrier(jnp.mean(shaped * shaped, axis=-1, keepdims=True)) + 1e-06)
    return normal.astype(jnp.bfloat16).reshape(values.shape[0], -1)

def reference(features, norm_gain, norm_bias, latent_kernel, latent_bias, token_mask, embed_weight, mask_token, pos_embed, query_weight, key_weight, value_weight, logit_scale, pattern):
    frames, slab_rows, row_width, channels = features.shape
    per_group = channels // GROUPS
    widened = features.astype(jnp.float32)
    grouped = widened.reshape(-1, GROUPS, per_group)
    totals = lax.optimization_barrier(jnp.sum(grouped, axis=(0, 2)))
    squares = lax.optimization_barrier(jnp.sum(grouped * grouped, axis=(0, 2)))
    cell_count = frames * slab_rows * row_width * per_group
    average = totals / cell_count
    variance = squares / cell_count - average * average
    inverse = lax.rsqrt(variance + 1e-06)
    channel_scale = jnp.repeat(inverse, per_group) * norm_gain
    channel_shift = norm_bias - jnp.repeat(average * inverse, per_group) * norm_gain
    activated = jax.nn.silu(widened * channel_scale + channel_shift).astype(jnp.bfloat16)
    padded = jnp.pad(activated, ((1, 1), (1, 1), (1, 1), (0, 0)))
    summed = jnp.zeros((frames * slab_rows * row_width, LAT), jnp.float32)
    for offset_t in range(3):
        for offset_h in range(3):
            for offset_w in range(3):
                window = padded[offset_t:offset_t + frames, offset_h:offset_h + slab_rows, offset_w:offset_w + row_width]
                summed = summed + jnp.dot(window.reshape(-1, channels), latent_kernel[:, offset_t, offset_h, offset_w, :].T, preferred_element_type=jnp.float32)
    latent = (summed + latent_bias).astype(jnp.bfloat16)
    tokens = jnp.dot(latent, embed_weight, preferred_element_type=jnp.float32)
    tokens = jnp.where(token_mask.reshape(-1, 1) == 1, mask_token, tokens)
    tokens = tokens + pos_embed.reshape(-1, pos_embed.shape[-1]).astype(jnp.float32)
    centred = tokens - lax.optimization_barrier(jnp.mean(tokens, axis=-1, keepdims=True))
    hidden = (centred * lax.rsqrt(lax.optimization_barrier(jnp.mean(centred * centred, axis=-1, keepdims=True)) + 1e-05)).astype(jnp.bfloat16)
    unit_query = unit_heads(jnp.dot(hidden, query_weight, preferred_element_type=jnp.float32).astype(jnp.bfloat16), HEADS)
    unit_key = unit_heads(jnp.dot(hidden, key_weight, preferred_element_type=jnp.float32).astype(jnp.bfloat16), HEADS)
    value_raw = jnp.dot(hidden, value_weight, preferred_element_type=jnp.float32).astype(jnp.bfloat16)
    pair_total = slab_rows // 2
    block_span = 2 * row_width
    inner = HEADS * HD
    query_blocks = unit_query.reshape(frames, pair_total, block_span, HEADS, HD)
    key_blocks = unit_key.reshape(frames * pair_total, block_span, inner)
    value_blocks = value_raw.reshape(frames * pair_total, block_span, inner)
    scale = logit_scale / HD

    def one_frame(inputs):
        frame_queries, frame_list = inputs
        usable = frame_list >= 0
        clamped = jnp.maximum(frame_list, 0)
        key_rows = jnp.take(key_blocks, clamped, axis=0).reshape(pair_total, MAXKB * block_span, HEADS, HD).astype(jnp.float32)
        value_rows = jnp.take(value_blocks, clamped, axis=0).reshape(pair_total, MAXKB * block_span, HEADS, HD).astype(jnp.float32)
        scores = jnp.einsum('bqhd,bkhd->bhqk', frame_queries.astype(jnp.float32), key_rows) * scale[None, :, None, None]
        live_keys = jnp.repeat(usable, block_span, axis=1).astype(jnp.float32)
        weights = jnp.exp(scores) * live_keys[:, None, None, :]
        denominator = lax.optimization_barrier(jnp.sum(weights, axis=-1))
        rounded = lax.optimization_barrier(weights.astype(jnp.bfloat16)).astype(jnp.float32)
        numerator = jnp.einsum('bhqk,bkhd->bqhd', rounded, value_rows)
        return (numerator / jnp.transpose(denominator, (0, 2, 1))[..., None]).astype(jnp.bfloat16)
    attended = lax.map(one_frame, (query_blocks, pattern))
    return attended.reshape(frames, slab_rows, row_width, inner)
```

```python
import functools

import jax
import jax.numpy as jnp
from jax import lax
from jax.experimental import pallas as pl
from jax.experimental.pallas import tpu as pltpu
from jax.sharding import PartitionSpec as P

MESH = pl.DeviceIdType.MESH
F32, BF16 = jnp.float32, jnp.bfloat16
GROUP = 16
NT_DIMS = (((1,), (1,)), ((), ()))
TN_DIMS = (((0,), (0,)), ((), ()))
MIB = 1 << 20


def remote(src, dst, send, recv, tm, row):
    return pltpu.make_async_remote_copy(
        src_ref=src,
        dst_ref=dst,
        send_sem=send,
        recv_sem=recv,
        device_id={"tm": tm, "row": row},
        device_id_type=MESH,
    )


def group_sum(x):
    lane = lax.broadcasted_iota(jnp.int32, x.shape, 1)
    for k in (1, 2, 4, 8):
        down = pltpu.roll(x, 128 - k, 1)
        up = pltpu.roll(x, k, 1)
        x = x + jnp.where((lane & k) == 0, down, up)
    return x


def mask_rows(mask_token):
    hi = mask_token.astype(BF16).astype(F32)
    mid = (mask_token - hi).astype(BF16).astype(F32)
    low = mask_token - hi - mid
    row = lax.broadcasted_iota(jnp.int32, (16, mask_token.shape[1]), 0)
    zero = jnp.zeros(row.shape, F32)
    return jnp.where(row == 0, hi, jnp.where(row == 1, mid, jnp.where(row == 2, low, zero))).astype(BF16)


def layer_norm(tokens, pos):
    x = tokens + pos.astype(F32)
    c = x - jnp.mean(x, axis=-1, keepdims=True)
    return (c * lax.rsqrt(jnp.mean(c * c, axis=-1, keepdims=True) + 1e-05)).astype(BF16)


def head_norm(y):
    y = y.astype(BF16).astype(F32)
    parts = []
    for i in range(y.shape[1] // 128):
        part = y[:, 128 * i : 128 * (i + 1)]
        parts.append(part * lax.rsqrt(jnp.mean(part * part, axis=-1, keepdims=True) + 1e-06))
    return jnp.concatenate(parts, axis=1).astype(BF16)


def front(
    tm_n, row_n,
    feat, aux, taps, embed, mask_token, pos, wq, wk, wv,
    q_out, k_out, v_out, pos_halo, lat_halo,
    cells, act, aux_v, taps_v, emb_v, mtok_v, pos_v, w_v, hidden, tok, lat, qkv, mine, stat_r, stat_t, affine,
    load, f_send, f_recv, r_send, r_recv, t_send, t_recv, p_send, p_recv, c_send, c_recv, l_send, l_recv,
):
    tm, row = lax.axis_index("tm"), lax.axis_index("row")

    def wrap(i, n):
        return lax.rem(i + n, n)

    before, after = wrap(tm - 1, tm_n), wrap(tm + 1, tm_n)
    above, below = wrap(row - 1, row_n), wrap(row + 1, row_n)

    own = pltpu.make_async_copy(feat, cells.at[1:5, 1:5], load.at[0])
    own.start()
    local = [
        pltpu.make_async_copy(aux, aux_v, load.at[1]),
        pltpu.make_async_copy(taps, taps_v, load.at[2]),
        pltpu.make_async_copy(embed, emb_v.at[0:16], load.at[3]),
        pltpu.make_async_copy(mask_token, mtok_v, load.at[4]),
        pltpu.make_async_copy(pos, pos_v, load.at[5]),
        pltpu.make_async_copy(wq, w_v.at[0], load.at[6]),
        pltpu.make_async_copy(wk, w_v.at[1], load.at[7]),
        pltpu.make_async_copy(wv, w_v.at[2], load.at[8]),
    ]
    for copy in local:
        copy.start()

    barrier = pltpu.get_barrier_semaphore()
    for d in range(1, row_n):
        pl.semaphore_signal(barrier, inc=1, device_id={"tm": tm, "row": wrap(row + d, row_n)}, device_id_type=MESH)
    for d in range(1, tm_n):
        pl.semaphore_signal(barrier, inc=1, device_id={"tm": wrap(tm + d, tm_n), "row": row}, device_id_type=MESH)
    for t in (before, after):
        for r in (above, below):
            pl.semaphore_signal(barrier, inc=1, device_id={"tm": t, "row": r}, device_id_type=MESH)
    pl.semaphore_wait(barrier, row_n - 1 + tm_n - 1 + 4)

    halo = [
        (feat.at[:, 3], cells.at[1:5, 0], tm, below),
        (feat.at[:, 0], cells.at[1:5, 5], tm, above),
        (feat.at[3], cells.at[0, 1:5], after, row),
        (feat.at[0], cells.at[5, 1:5], before, row),
        (feat.at[3, 3], cells.at[0, 0], after, below),
        (feat.at[3, 0], cells.at[0, 5], after, above),
        (feat.at[0, 3], cells.at[5, 0], before, below),
        (feat.at[0, 0], cells.at[5, 5], before, above),
    ]
    feat_copies = [
        remote(src, dst, f_send.at[i], f_recv.at[i], t, r) for i, (src, dst, t, r) in enumerate(halo)
    ]
    for copy in feat_copies:
        copy.start()

    own.wait()
    half = jnp.zeros((8, 512), F32)

    def add_row(i, carry):
        total, square = carry
        x = cells[1 + i // 4, 1 + i % 4].astype(F32)
        for j in range(8):
            part = x[8 * j : 8 * (j + 1)]
            total, square = total + part, square + part * part
        return total, square

    total, square = lax.fori_loop(0, 16, add_row, (half, half))
    total = jnp.sum(total, axis=0, keepdims=True)
    square = jnp.sum(square, axis=0, keepdims=True)
    for i in range(4):
        mine[0, i : i + 1] = total[:, 128 * i : 128 * (i + 1)]
        mine[0, 4 + i : 5 + i] = square[:, 128 * i : 128 * (i + 1)]
    row_copies = [
        remote(mine.at[0], stat_r.at[d - 1], r_send.at[d - 1], r_recv.at[d - 1], tm, wrap(row + d, row_n))
        for d in range(1, row_n)
    ]
    for copy in row_copies:
        copy.start()
    for copy in row_copies:
        copy.wait_recv()
    mine[1] = mine[0] + jnp.sum(stat_r[...], axis=0)
    tm_copies = [
        remote(mine.at[1], stat_t.at[d - 1], t_send.at[d - 1], t_recv.at[d - 1], wrap(tm + d, tm_n), row)
        for d in range(1, tm_n)
    ]
    for copy in tm_copies:
        copy.start()
    for copy in tm_copies:
        copy.wait_recv()

    pos_copies = {}
    for i, t in enumerate((0, 3, 1, 2)):
        pos_copies["down", t] = remote(pos.at[2 * t + 1], pos_halo.at[1 + t, 0], p_send.at[i], p_recv.at[i], tm, below)
        pos_copies["up", t] = remote(pos.at[2 * t], pos_halo.at[1 + t, 3], p_send.at[4 + i], p_recv.at[4 + i], tm, above)
    pos_copies["after", 0] = remote(pos.at[6:8], pos_halo.at[0, 1:3], p_send.at[8], p_recv.at[8], after, row)
    pos_copies["before", 0] = remote(pos.at[0:2], pos_halo.at[5, 1:3], p_send.at[9], p_recv.at[9], before, row)
    for copy in pos_copies.values():
        copy.start()

    for copy in local[:5]:
        copy.wait()
    every = group_sum(mine[1] + jnp.sum(stat_t[...], axis=0))
    count = tm_n * row_n * 4 * 4 * 64 * GROUP
    average = every[0:4] / count
    variance = every[4:8] / count - average * average
    inverse = lax.rsqrt(variance + 1e-06)
    affine[0:4] = inverse * aux_v[0:4]
    affine[4:8] = aux_v[4:8] - average * inverse * aux_v[0:4]
    emb_v[16:32] = mask_rows(mtok_v[...])

    for copy in feat_copies:
        copy.wait_recv()

    def activate(i, _):
        f, r = i // 6, i % 6
        frame, line = tm * 4 + f - 1, row * 4 + r - 1
        inside = (frame >= 0) & (frame < tm_n * 4) & (line >= 0) & (line < row_n * 4)
        keep = jnp.where(inside, 0.5, 0.0)
        for j in range(4):
            lanes = slice(128 * j, 128 * (j + 1))
            v = cells[f, r, :, lanes].astype(F32) * affine[j : j + 1] + affine[4 + j : 5 + j]
            v = (v * keep) * (1.0 + jnp.tanh(0.5 * v))
            act[f, pl.ds(pl.multiple_of(r * 64, 64), 64), lanes] = v.astype(BF16)
        return 0

    lax.fori_loop(0, 36, activate, 0)

    column = lax.broadcasted_iota(jnp.int32, (16, 256), 1) % 64
    third = lax.broadcasted_iota(jnp.int32, (16, 128), 0) < 3

    def convolve(t, _):
        acc = jnp.zeros((144, 384), F32)
        for a in range(3):
            acc = acc + lax.dot_general(taps_v[a], act[t + a], NT_DIMS, preferred_element_type=F32)
        sums = []
        for c in range(3):
            part = acc[16 * c : 16 * c + 16]
            for b in (1, 2):
                part = part + pltpu.roll(acc[48 * b + 16 * c : 48 * b + 16 * c + 16], 384 - 64 * b, 1)
            sums.append(part[:, :256])
        left = jnp.where(column == 0, 0.0, pltpu.roll(sums[0], 1, 1))
        right = jnp.where(column == 63, 0.0, pltpu.roll(sums[2], 255, 1))
        out = sums[1] + left + right
        for p in range(2):
            masked = aux_v[pl.ds(24 + 2 * t + p, 1)]
            value = (out[:, 128 * p : 128 * (p + 1)] + aux_v[8:24]).astype(BF16).astype(F32)
            lat[2 * t + p, 0:16] = jnp.where(masked > 0.5, 0.0, value).astype(BF16)
            lat[2 * t + p, 16:32] = jnp.where(third, masked, 0.0).astype(BF16)
        return 0

    lax.fori_loop(0, 4, convolve, 0)

    lat_sends = []
    for t in range(4):
        lat_sends.append((lat.at[2 * t + 1], lat_halo.at[1 + t, 0], tm, below))
        lat_sends.append((lat.at[2 * t], lat_halo.at[1 + t, 3], tm, above))
    lat_sends += [
        (lat.at[6:8], lat_halo.at[0, 1:3], after, row),
        (lat.at[0:2], lat_halo.at[5, 1:3], before, row),
        (lat.at[7], lat_halo.at[0, 0], after, below),
        (lat.at[6], lat_halo.at[0, 3], after, above),
        (lat.at[1], lat_halo.at[5, 0], before, below),
        (lat.at[0], lat_halo.at[5, 3], before, above),
    ]
    lat_copies = [remote(src, dst, l_send.at[i], l_recv.at[i], t, r) for i, (src, dst, t, r) in enumerate(lat_sends)]
    for copy in lat_copies:
        copy.start()

    def normalize(j, _):
        tok[...] = lax.dot_general(lat[j], emb_v[...], TN_DIMS, preferred_element_type=F32)

        def piece(i, _):
            rows = pl.ds(pl.multiple_of(i * 16, 16), 16)
            hidden[pl.ds(pl.multiple_of(j * 128 + i * 16, 16), 16)] = layer_norm(tok[rows], pos_v[j, rows])
            return 0

        lax.fori_loop(0, 8, piece, 0)
        return 0

    lax.fori_loop(0, 8, normalize, 0)

    def project(n, normed):
        def tile(i, _):
            m, c = i // 4, i % 4
            columns = pl.ds(pl.multiple_of(c * 256, 256), 256)
            y = jnp.dot(
                hidden[pl.ds(pl.multiple_of(m * 512, 512), 512)], w_v[n, :, columns], preferred_element_type=F32
            )
            y = head_norm(y) if normed else y.astype(BF16)
            qkv[n, pl.ds(m * 4, 4), :, columns] = y.reshape(4, 128, 256)
            return 0

        lax.fori_loop(0, 8, tile, 0)

    stores = [pltpu.make_async_copy(qkv.at[n], out, load.at[9 + n]) for n, out in enumerate((q_out, k_out, v_out))]
    local[5].wait()
    project(0, True)
    stores[0].start()

    odd = lax.rem(row, 2)
    other = row + 1 - 2 * odd
    outer = 3 * odd
    inner_src = 2 - odd
    for t in (0, 3):
        pos_copies["down", t].wait_recv()
        pos_copies["up", t].wait_recv()
    pos_copies["after", 0].wait_recv()
    pos_copies["before", 0].wait_recv()
    corner = [
        remote(pos_halo.at[1, outer], pos_halo.at[5, outer], c_send.at[0], c_recv.at[0], before, row),
        remote(pos_halo.at[4, outer], pos_halo.at[0, outer], c_send.at[1], c_recv.at[1], after, row),
        remote(pos_halo.at[0, inner_src], pos_halo.at[0, outer], c_send.at[2], c_recv.at[2], tm, other),
        remote(pos_halo.at[5, inner_src], pos_halo.at[5, outer], c_send.at[3], c_recv.at[3], tm, other),
    ]
    for copy in corner:
        copy.start()

    local[6].wait()
    project(1, True)
    stores[1].start()
    local[7].wait()
    project(2, False)
    stores[2].start()

    for t in (1, 2):
        pos_copies["down", t].wait_recv()
        pos_copies["up", t].wait_recv()
    for copy in [*lat_copies, *corner]:
        copy.wait_recv()
    for copy in [*feat_copies, *row_copies, *tm_copies, *pos_copies.values(), *lat_copies, *corner]:
        copy.wait_send()
    for copy in stores:
        copy.wait()


def back(
    tm_n, row_n,
    pattern, scale, q, k, v, pos_halo, lat_halo, embed, mask_token, wk, wv,
    out,
    place, need, q_v, k_v, v_v, lat_v, emb_v, mtok_v, w_v, pos_v, tok, hidden, out_v,
    load, p_sem, o_sem,
):
    tm, row = lax.axis_index("tm"), lax.axis_index("row")
    copies = [
        pltpu.make_async_copy(lat_halo, lat_v, load.at[0]),
        pltpu.make_async_copy(embed, emb_v.at[0:16], load.at[1]),
        pltpu.make_async_copy(mask_token, mtok_v, load.at[2]),
        pltpu.make_async_copy(wk, w_v.at[0], load.at[3]),
        pltpu.make_async_copy(wv, w_v.at[1], load.at[4]),
        pltpu.make_async_copy(q, q_v, load.at[5]),
    ]
    for t in range(4):
        copies.append(pltpu.make_async_copy(k.at[2 * t : 2 * t + 2], k_v.at[4 * t + 5 : 4 * t + 7], load.at[6 + t]))
        copies.append(pltpu.make_async_copy(v.at[2 * t : 2 * t + 2], v_v.at[4 * t + 5 : 4 * t + 7], load.at[10 + t]))
    for copy in copies:
        copy.start()

    def clear(i, _):
        need[i] = 0
        return 0

    lax.fori_loop(0, 24, clear, 0)

    def visit(i, _):
        b, s = i // 4, i % 4
        block = pattern[b, s]
        spot = ((block // (2 * row_n)) - tm * 4 + 1) * 4 + (block % (2 * row_n)) - row * 2 + 1
        spot = jnp.where(block >= 0, spot, 5)
        place[i] = spot
        need[spot] = 1
        return 0

    lax.fori_loop(0, 32, visit, 0)

    def gather(i, n):
        f, p = i // 4, i % 4
        own = (f >= 1) & (f <= 4) & (p >= 1) & (p <= 2)
        wanted = (need[i] == 1) & jnp.logical_not(own)

        @pl.when(wanted)
        def _():
            need[24 + n] = i
            pltpu.make_async_copy(pos_halo.at[f, p], pos_v.at[n], p_sem.at[n]).start()

        return n + jnp.where(wanted, 1, 0)

    n = lax.fori_loop(0, 24, gather, 0)

    for copy in copies[:5]:
        copy.wait()
    emb_v[16:32] = mask_rows(mtok_v[...])

    def pair(g, _):
        for u in range(2):
            i = 2 * g + u
            at = jnp.minimum(i, n - 1)
            spot = need[24 + at]

            @pl.when(i < n)
            def _():
                pltpu.make_async_copy(pos_halo.at[0, 0], pos_v.at[at], p_sem.at[at]).wait()

            tok[...] = lax.dot_general(lat_v[spot // 4, spot % 4], emb_v[...], TN_DIMS, preferred_element_type=F32)

            def piece(c, _):
                rows = pl.ds(pl.multiple_of(c * 16, 16), 16)
                hidden[pl.ds(pl.multiple_of(u * 128 + c * 16, 16), 16)] = layer_norm(tok[rows], pos_v[at, rows])
                return 0

            lax.fori_loop(0, 8, piece, 0)
        first = need[24 + 2 * g]
        second = need[24 + jnp.minimum(2 * g + 1, n - 1)]

        def tile(c, _):
            columns = pl.ds(pl.multiple_of(c * 256, 256), 256)
            y = head_norm(jnp.dot(hidden[...], w_v[0, :, columns], preferred_element_type=F32))
            k_v[first, :, columns] = y[0:128]
            k_v[second, :, columns] = y[128:256]
            y = jnp.dot(hidden[...], w_v[1, :, columns], preferred_element_type=F32).astype(BF16)
            v_v[first, :, columns] = y[0:128]
            v_v[second, :, columns] = y[128:256]
            return 0

        lax.fori_loop(0, 4, tile, 0)
        return 0

    lax.fori_loop(0, (n + 1) // 2, pair, 0)
    for copy in copies[5:]:
        copy.wait()

    def attend(b, live):
        spots = [place[4 * b + s] for s in range(live)]

        def head(h, _):
            columns = pl.ds(pl.multiple_of(h * 128, 128), 128)
            query = q_v[b, :, columns]
            factor = scale[h] / 128.0
            total = acc = None
            for spot in spots:
                score = lax.dot_general(query, k_v[spot, :, columns], NT_DIMS, preferred_element_type=F32)
                weight = jnp.exp(score * factor)
                part = jnp.dot(weight.astype(BF16), v_v[spot, :, columns], preferred_element_type=F32)
                total = weight if total is None else total + weight
                acc = part if acc is None else acc + part
            out_v[b, :, columns] = (acc / jnp.sum(total, axis=-1, keepdims=True)).astype(BF16)
            return 0

        lax.fori_loop(0, 8, head, 0, unroll=4)

    def block(b, _):
        live = sum((pattern[b, s] >= 0).astype(jnp.int32) for s in range(4))
        for count in range(1, 5):
            pl.when(live == count)(functools.partial(attend, b, count))
        pltpu.make_async_copy(out_v.at[b], out.at[b], o_sem.at[b]).start()
        return 0

    lax.fori_loop(0, 8, block, 0)
    for b in range(8):
        pltpu.make_async_copy(out_v.at[b], out.at[b], o_sem.at[b]).wait()


def per_device(
    tm_n, row_n,
    features, norm_gain, norm_bias, latent_kernel, latent_bias, token_mask, embed_weight, mask_token, pos_embed,
    query_weight, key_weight, value_weight, logit_scale, pattern,
):
    taps = latent_kernel.transpose(1, 2, 3, 0, 4).reshape(3, 144, 512)
    aux = jnp.concatenate(
        [
            norm_gain.reshape(4, 128),
            norm_bias.reshape(4, 128),
            jnp.broadcast_to(latent_bias[:, None], (16, 128)),
            token_mask.reshape(8, 128).astype(F32),
        ]
    )
    pos = pos_embed.reshape(8, 128, 2048)
    mtok = mask_token.reshape(1, 2048)
    anywhere = pl.BlockSpec(memory_space=pl.ANY)
    dma = pltpu.SemaphoreType.DMA
    block = jax.ShapeDtypeStruct((8, 128, 1024), BF16)
    q, k, v, pos_halo, lat_halo = pl.pallas_call(
        functools.partial(front, tm_n, row_n),
        name="front",
        out_shape=[
            block, block, block,
            jax.ShapeDtypeStruct((6, 4, 128, 2048), BF16),
            jax.ShapeDtypeStruct((6, 4, 32, 128), BF16),
        ],
        in_specs=[anywhere] * 9,
        out_specs=[anywhere] * 5,
        scratch_shapes=[
            pltpu.VMEM((6, 6, 64, 512), BF16),
            pltpu.VMEM((6, 384, 512), BF16),
            pltpu.VMEM((32, 128), F32),
            pltpu.VMEM((3, 144, 512), BF16),
            pltpu.VMEM((32, 2048), BF16),
            pltpu.VMEM((1, 2048), F32),
            pltpu.VMEM((8, 128, 2048), BF16),
            pltpu.VMEM((3, 2048, 1024), BF16),
            pltpu.VMEM((1024, 2048), BF16),
            pltpu.VMEM((128, 2048), F32),
            pltpu.VMEM((8, 32, 128), BF16),
            pltpu.VMEM((3, 8, 128, 1024), BF16),
            pltpu.VMEM((2, 8, 128), F32),
            pltpu.VMEM((row_n - 1, 8, 128), F32),
            pltpu.VMEM((tm_n - 1, 8, 128), F32),
            pltpu.VMEM((8, 128), F32),
            dma((12,)),
            dma((8,)), dma((8,)),
            dma((row_n - 1,)), dma((row_n - 1,)),
            dma((tm_n - 1,)), dma((tm_n - 1,)),
            dma((10,)), dma((10,)),
            dma((4,)), dma((4,)),
            dma((14,)), dma((14,)),
        ],
        compiler_params=pltpu.CompilerParams(
            collective_id=0, has_side_effects=True, vmem_limit_bytes=56 * MIB
        ),
    )(features, aux, taps, embed_weight, mtok, pos, query_weight, key_weight, value_weight)
    smem = pl.BlockSpec(memory_space=pltpu.SMEM)
    out = pl.pallas_call(
        functools.partial(back, tm_n, row_n),
        name="back",
        out_shape=block,
        in_specs=[smem, smem] + [anywhere] * 9,
        out_specs=anywhere,
        scratch_shapes=[
            pltpu.SMEM((32,), jnp.int32),
            pltpu.SMEM((48,), jnp.int32),
            pltpu.VMEM((8, 128, 1024), BF16),
            pltpu.VMEM((24, 128, 1024), BF16),
            pltpu.VMEM((24, 128, 1024), BF16),
            pltpu.VMEM((6, 4, 32, 128), BF16),
            pltpu.VMEM((32, 2048), BF16),
            pltpu.VMEM((1, 2048), F32),
            pltpu.VMEM((2, 2048, 1024), BF16),
            pltpu.VMEM((16, 128, 2048), BF16),
            pltpu.VMEM((128, 2048), F32),
            pltpu.VMEM((256, 2048), BF16),
            pltpu.VMEM((8, 128, 1024), BF16),
            dma((14,)), dma((16,)), dma((8,)),
        ],
        compiler_params=pltpu.CompilerParams(vmem_limit_bytes=56 * MIB),
    )(pattern.reshape(8, 4), logit_scale, q, k, v, pos_halo, lat_halo, embed_weight, mtok, key_weight, value_weight)
    return out.reshape(4, 4, 64, 1024)


def solution(mesh):
    slab = ("tm", "row")
    return jax.shard_map(
        functools.partial(per_device, mesh.shape["tm"], mesh.shape["row"]),
        mesh=mesh,
        in_specs=(
            P(*slab, None, None), P(), P(), P(), P(), P(*slab, None), P(), P(), P(*slab, None, None),
            P(), P(), P(), P(), P(*slab, None),
        ),
        out_specs=P(*slab, None, None),
        check_vma=False,
    )
```

```python
import functools

import jax
import jax.numpy as jnp
from jax import lax
from jax.experimental import pallas as pl
from jax.experimental.pallas import tpu as pltpu
from jax.sharding import PartitionSpec as P

MESH = pl.DeviceIdType.MESH
F32, BF16 = jnp.float32, jnp.bfloat16
GROUP = 16
NT_DIMS = (((1,), (1,)), ((), ()))
TN_DIMS = (((0,), (0,)), ((), ()))
MIB = 1 << 20


def remote(src, dst, send, recv, tm, row):
    return pltpu.make_async_remote_copy(
        src_ref=src,
        dst_ref=dst,
        send_sem=send,
        recv_sem=recv,
        device_id={"tm": tm, "row": row},
        device_id_type=MESH,
    )


def group_sum(x):
    lane = lax.broadcasted_iota(jnp.int32, x.shape, 1)
    for k in (1, 2, 4, 8):
        down = pltpu.roll(x, 128 - k, 1)
        up = pltpu.roll(x, k, 1)
        x = x + jnp.where((lane & k) == 0, down, up)
    return x


def mask_rows(mask_token):
    hi = mask_token.astype(BF16).astype(F32)
    mid = (mask_token - hi).astype(BF16).astype(F32)
    low = mask_token - hi - mid
    row = lax.broadcasted_iota(jnp.int32, (16, mask_token.shape[1]), 0)
    zero = jnp.zeros(row.shape, F32)
    return jnp.where(row == 0, hi, jnp.where(row == 1, mid, jnp.where(row == 2, low, zero))).astype(BF16)


def layer_norm(tokens, pos):
    x = tokens + pos.astype(F32)
    c = x - jnp.mean(x, axis=-1, keepdims=True)
    return (c * lax.rsqrt(jnp.mean(c * c, axis=-1, keepdims=True) + 1e-05)).astype(BF16)


def head_norm(y):
    y = y.astype(BF16).astype(F32)
    parts = []
    for i in range(y.shape[1] // 128):
        part = y[:, 128 * i : 128 * (i + 1)]
        parts.append(part * lax.rsqrt(jnp.mean(part * part, axis=-1, keepdims=True) + 1e-06))
    return jnp.concatenate(parts, axis=1).astype(BF16)


def layer(
    tm_n, row_n,
    pattern, scale, feat, aux, taps, embed, mask_token, pos, wq, wk, wv,
    out,
    cells, act, aux_v, taps_v, emb_v, mtok_v, pos_v, w_v, hidden_a, hidden_b, tok, lat_v, q_v, k_v, v_v, out_v,
    mine, stat_r, stat_t, affine,
    load, o_sem, f_send, f_recv, r_send, r_recv, t_send, t_recv, p_send, p_recv, c_send, c_recv, l_send, l_recv,
):
    tm, row = lax.axis_index("tm"), lax.axis_index("row")

    def wrap(i, n):
        return lax.rem(i + n, n)

    before, after = wrap(tm - 1, tm_n), wrap(tm + 1, tm_n)
    above, below = wrap(row - 1, row_n), wrap(row + 1, row_n)

    own = pltpu.make_async_copy(feat, cells.at[1:5, 1:5], load.at[0])
    own.start()
    local = [
        pltpu.make_async_copy(aux, aux_v, load.at[1]),
        pltpu.make_async_copy(taps, taps_v, load.at[2]),
        pltpu.make_async_copy(embed, emb_v.at[0:16], load.at[3]),
        pltpu.make_async_copy(mask_token, mtok_v, load.at[4]),
        *[
            pltpu.make_async_copy(pos.at[2 * t : 2 * t + 2], pos_v.at[4 * t + 5 : 4 * t + 7], load.at[5 + t])
            for t in range(4)
        ],
        pltpu.make_async_copy(wq, w_v.at[0], load.at[9]),
        pltpu.make_async_copy(wk, w_v.at[1], load.at[10]),
        pltpu.make_async_copy(wv, w_v.at[2], load.at[11]),
    ]
    for copy in local:
        copy.start()

    barrier = pltpu.get_barrier_semaphore()
    for d in range(1, row_n):
        pl.semaphore_signal(barrier, inc=1, device_id={"tm": tm, "row": wrap(row + d, row_n)}, device_id_type=MESH)
    for d in range(1, tm_n):
        pl.semaphore_signal(barrier, inc=1, device_id={"tm": wrap(tm + d, tm_n), "row": row}, device_id_type=MESH)
    for t in (before, after):
        for r in (above, below):
            pl.semaphore_signal(barrier, inc=1, device_id={"tm": t, "row": r}, device_id_type=MESH)
    pl.semaphore_wait(barrier, row_n - 1 + tm_n - 1 + 4)

    halo = [
        (feat.at[:, 3], cells.at[1:5, 0], tm, below),
        (feat.at[:, 0], cells.at[1:5, 5], tm, above),
        (feat.at[3], cells.at[0, 1:5], after, row),
        (feat.at[0], cells.at[5, 1:5], before, row),
        (feat.at[3, 3], cells.at[0, 0], after, below),
        (feat.at[3, 0], cells.at[0, 5], after, above),
        (feat.at[0, 3], cells.at[5, 0], before, below),
        (feat.at[0, 0], cells.at[5, 5], before, above),
    ]
    feat_copies = [
        remote(src, dst, f_send.at[i], f_recv.at[i], t, r) for i, (src, dst, t, r) in enumerate(halo)
    ]
    for copy in feat_copies:
        copy.start()

    own.wait()
    half = jnp.zeros((8, 512), F32)

    def add_row(i, carry):
        total, square = carry
        x = cells[1 + i // 4, 1 + i % 4].astype(F32)
        for j in range(8):
            part = x[8 * j : 8 * (j + 1)]
            total, square = total + part, square + part * part
        return total, square

    total, square = lax.fori_loop(0, 16, add_row, (half, half))
    total = jnp.sum(total, axis=0, keepdims=True)
    square = jnp.sum(square, axis=0, keepdims=True)
    for i in range(4):
        mine[0, i : i + 1] = total[:, 128 * i : 128 * (i + 1)]
        mine[0, 4 + i : 5 + i] = square[:, 128 * i : 128 * (i + 1)]
    row_copies = [
        remote(mine.at[0], stat_r.at[d - 1], r_send.at[d - 1], r_recv.at[d - 1], tm, wrap(row + d, row_n))
        for d in range(1, row_n)
    ]
    for copy in row_copies:
        copy.start()
    for copy in row_copies:
        copy.wait_recv()
    mine[1] = mine[0] + jnp.sum(stat_r[...], axis=0)
    tm_copies = [
        remote(mine.at[1], stat_t.at[d - 1], t_send.at[d - 1], t_recv.at[d - 1], wrap(tm + d, tm_n), row)
        for d in range(1, tm_n)
    ]
    for copy in tm_copies:
        copy.start()
    for copy in tm_copies:
        copy.wait_recv()

    down, up = {}, {}
    for i, t in enumerate((0, 3, 1, 2)):
        down[t] = remote(pos.at[2 * t + 1], pos_v.at[4 * t + 4], p_send.at[i], p_recv.at[i], tm, below)
        up[t] = remote(pos.at[2 * t], pos_v.at[4 * t + 7], p_send.at[4 + i], p_recv.at[4 + i], tm, above)
    along = [
        remote(pos.at[6:8], pos_v.at[1:3], p_send.at[8], p_recv.at[8], after, row),
        remote(pos.at[0:2], pos_v.at[21:23], p_send.at[9], p_recv.at[9], before, row),
    ]
    first = [down[0], up[0], down[3], up[3], *along]
    second = [down[1], up[1], down[2], up[2]]
    for copy in first:
        copy.start()

    for copy in local[:5]:
        copy.wait()
    every = group_sum(mine[1] + jnp.sum(stat_t[...], axis=0))
    count = tm_n * row_n * 4 * 4 * 64 * GROUP
    average = every[0:4] / count
    variance = every[4:8] / count - average * average
    inverse = lax.rsqrt(variance + 1e-06)
    affine[0:4] = inverse * aux_v[0:4]
    affine[4:8] = aux_v[4:8] - average * inverse * aux_v[0:4]
    emb_v[16:32] = mask_rows(mtok_v[...])

    for copy in feat_copies:
        copy.wait_recv()

    def activate(i, _):
        f, r = i // 6, i % 6
        frame, line = tm * 4 + f - 1, row * 4 + r - 1
        inside = (frame >= 0) & (frame < tm_n * 4) & (line >= 0) & (line < row_n * 4)
        keep = jnp.where(inside, 0.5, 0.0)
        for j in range(4):
            lanes = slice(128 * j, 128 * (j + 1))
            v = cells[f, r, :, lanes].astype(F32) * affine[j : j + 1] + affine[4 + j : 5 + j]
            v = (v * keep) * (1.0 + jnp.tanh(0.5 * v))
            act[f, pl.ds(pl.multiple_of(r * 64, 64), 64), lanes] = v.astype(BF16)
        return 0

    lax.fori_loop(0, 36, activate, 0)

    column = lax.broadcasted_iota(jnp.int32, (16, 256), 1) % 64
    third = lax.broadcasted_iota(jnp.int32, (16, 128), 0) < 3

    def convolve(t, _):
        acc = jnp.zeros((144, 384), F32)
        for a in range(3):
            acc = acc + lax.dot_general(taps_v[a], act[t + a], NT_DIMS, preferred_element_type=F32)
        sums = []
        for c in range(3):
            part = acc[16 * c : 16 * c + 16]
            for b in (1, 2):
                part = part + pltpu.roll(acc[48 * b + 16 * c : 48 * b + 16 * c + 16], 384 - 64 * b, 1)
            sums.append(part[:, :256])
        left = jnp.where(column == 0, 0.0, pltpu.roll(sums[0], 1, 1))
        right = jnp.where(column == 63, 0.0, pltpu.roll(sums[2], 255, 1))
        out = sums[1] + left + right
        for p in range(2):
            masked = aux_v[pl.ds(24 + 2 * t + p, 1)]
            value = (out[:, 128 * p : 128 * (p + 1)] + aux_v[8:24]).astype(BF16).astype(F32)
            lat_v[4 * t + 5 + p, 0:16] = jnp.where(masked > 0.5, 0.0, value).astype(BF16)
            lat_v[4 * t + 5 + p, 16:32] = jnp.where(third, masked, 0.0).astype(BF16)
        return 0

    lax.fori_loop(0, 4, convolve, 0)

    lat_sends = []
    for t in range(4):
        lat_sends.append((lat_v.at[4 * t + 6], lat_v.at[4 * t + 4], tm, below))
        lat_sends.append((lat_v.at[4 * t + 5], lat_v.at[4 * t + 7], tm, above))
    lat_sends += [
        (lat_v.at[17:19], lat_v.at[1:3], after, row),
        (lat_v.at[5:7], lat_v.at[21:23], before, row),
        (lat_v.at[18], lat_v.at[0], after, below),
        (lat_v.at[17], lat_v.at[3], after, above),
        (lat_v.at[6], lat_v.at[20], before, below),
        (lat_v.at[5], lat_v.at[23], before, above),
    ]
    lat_copies = [remote(src, dst, l_send.at[i], l_recv.at[i], t, r) for i, (src, dst, t, r) in enumerate(lat_sends)]
    for copy in lat_copies:
        copy.start()
    for copy in second:
        copy.start()

    def spot_of(group, i):
        base, a, b = group
        return base + a * (i % 2) + b * (i // 2)

    def normalize(group, i, hidden):
        spot = spot_of(group, i)
        tok[...] = lax.dot_general(lat_v[spot], emb_v[...], TN_DIMS, preferred_element_type=F32)
        for c in range(4):
            rows = slice(32 * c, 32 * c + 32)
            hidden[pl.ds(pl.multiple_of(i * 128 + 32 * c, 32), 32)] = layer_norm(tok[rows], pos_v[spot, rows])

    def project(group, following, hidden, other, own):
        spots = [spot_of(group, j) for j in range(4)]

        def step(i, _):
            columns = pl.ds(pl.multiple_of(i * 256, 256), 256)
            if following is not None:
                normalize(following, i, other)
            if own is not None:
                y = head_norm(jnp.dot(hidden[...], w_v[0, :, columns], preferred_element_type=F32))
                q_v[4 * own : 4 * own + 4, :, columns] = y.reshape(4, 128, 256)
            y = head_norm(jnp.dot(hidden[...], w_v[1, :, columns], preferred_element_type=F32))
            for j in range(4):
                k_v[spots[j], :, columns] = y[128 * j : 128 * (j + 1)]
            y = jnp.dot(hidden[...], w_v[2, :, columns], preferred_element_type=F32).astype(BF16)
            for j in range(4):
                v_v[spots[j], :, columns] = y[128 * j : 128 * (j + 1)]
            return 0

        lax.fori_loop(0, 4, step, 0)

    own_0, own_1, sides = (5, 1, 4), (13, 1, 4), (1, 1, 20)
    ends, corners, middle = (4, 3, 12), (0, 3, 20), (8, 3, 4)
    for copy in local[5:]:
        copy.wait()

    def begin(i, _):
        normalize(own_0, i, hidden_a)
        return 0

    lax.fori_loop(0, 4, begin, 0)
    project(own_0, own_1, hidden_a, hidden_b, 0)
    for copy in [*along, *lat_copies]:
        copy.wait_recv()
    project(own_1, sides, hidden_b, hidden_a, 1)

    odd = lax.rem(row, 2)
    other = row + 1 - 2 * odd
    outer = 3 * odd
    for copy in first[:4]:
        copy.wait_recv()
    corner = [
        remote(pos_v.at[4 + outer], pos_v.at[20 + outer], c_send.at[0], c_recv.at[0], before, row),
        remote(pos_v.at[16 + outer], pos_v.at[outer], c_send.at[1], c_recv.at[1], after, row),
        remote(pos_v.at[2 - odd], pos_v.at[outer], c_send.at[2], c_recv.at[2], tm, other),
        remote(pos_v.at[22 - odd], pos_v.at[20 + outer], c_send.at[3], c_recv.at[3], tm, other),
    ]
    for copy in corner:
        copy.start()
    project(sides, ends, hidden_a, hidden_b, None)
    for copy in corner:
        copy.wait_recv()
    project(ends, corners, hidden_b, hidden_a, None)
    for copy in second:
        copy.wait_recv()
    project(corners, middle, hidden_a, hidden_b, None)
    project(middle, None, hidden_b, hidden_a, None)

    def attend(b, _):
        mine_at = 4 * (b // 2) + 5 + b % 2
        spots, live = [], []
        for s in range(4):
            listed = pattern[b, s]
            spot = (listed // (2 * row_n) - tm * 4 + 1) * 4 + listed % (2 * row_n) - row * 2 + 1
            spots.append(jnp.clip(jnp.where(listed >= 0, spot, mine_at), 0, 23))
            live.append(jnp.where(listed >= 0, 1.0, 0.0))

        def head(h, _):
            columns = pl.ds(pl.multiple_of(h * 128, 128), 128)
            keys = jnp.concatenate([k_v[spot, :, columns] for spot in spots], axis=0)
            values = jnp.concatenate([v_v[spot, :, columns] for spot in spots], axis=0)
            score = lax.dot_general(q_v[b, :, columns], keys, NT_DIMS, preferred_element_type=F32)
            factor = scale[h] / 128.0
            parts = [jnp.exp(score[:, 128 * s : 128 * (s + 1)] * factor) * live[s] for s in range(4)]
            total = jnp.sum((parts[0] + parts[1]) + (parts[2] + parts[3]), axis=-1, keepdims=True)
            weight = jnp.concatenate([part.astype(BF16) for part in parts], axis=1)
            acc = jnp.dot(weight, values, preferred_element_type=F32)
            out_v[b, :, columns] = (acc / total).astype(BF16)
            return 0

        lax.fori_loop(0, 8, head, 0, unroll=4)
        pltpu.make_async_copy(out_v.at[b], out.at[b], o_sem.at[b]).start()
        return 0

    lax.fori_loop(0, 8, attend, 0)
    for copy in [*feat_copies, *row_copies, *tm_copies, *first, *second, *lat_copies, *corner]:
        copy.wait_send()
    for b in range(8):
        pltpu.make_async_copy(out_v.at[b], out.at[b], o_sem.at[b]).wait()


def per_device(
    tm_n, row_n,
    features, norm_gain, norm_bias, latent_kernel, latent_bias, token_mask, embed_weight, mask_token, pos_embed,
    query_weight, key_weight, value_weight, logit_scale, pattern,
):
    taps = latent_kernel.transpose(1, 2, 3, 0, 4).reshape(3, 144, 512)
    aux = jnp.concatenate(
        [
            norm_gain.reshape(4, 128),
            norm_bias.reshape(4, 128),
            jnp.broadcast_to(latent_bias[:, None], (16, 128)),
            token_mask.reshape(8, 128).astype(F32),
        ]
    )
    pos = pos_embed.reshape(8, 128, 2048)
    mtok = mask_token.reshape(1, 2048)
    anywhere = pl.BlockSpec(memory_space=pl.ANY)
    dma = pltpu.SemaphoreType.DMA
    block = jax.ShapeDtypeStruct((8, 128, 1024), BF16)
    smem = pl.BlockSpec(memory_space=pltpu.SMEM)
    out = pl.pallas_call(
        functools.partial(layer, tm_n, row_n),
        name="layer",
        out_shape=block,
        in_specs=[smem, smem] + [anywhere] * 9,
        out_specs=anywhere,
        scratch_shapes=[
            pltpu.VMEM((6, 6, 64, 512), BF16),
            pltpu.VMEM((6, 384, 512), BF16),
            pltpu.VMEM((32, 128), F32),
            pltpu.VMEM((3, 144, 512), BF16),
            pltpu.VMEM((32, 2048), BF16),
            pltpu.VMEM((1, 2048), F32),
            pltpu.VMEM((24, 128, 2048), BF16),
            pltpu.VMEM((3, 2048, 1024), BF16),
            pltpu.VMEM((512, 2048), BF16),
            pltpu.VMEM((512, 2048), BF16),
            pltpu.VMEM((128, 2048), F32),
            pltpu.VMEM((24, 32, 128), BF16),
            pltpu.VMEM((8, 128, 1024), BF16),
            pltpu.VMEM((24, 128, 1024), BF16),
            pltpu.VMEM((24, 128, 1024), BF16),
            pltpu.VMEM((8, 128, 1024), BF16),
            pltpu.VMEM((2, 8, 128), F32),
            pltpu.VMEM((row_n - 1, 8, 128), F32),
            pltpu.VMEM((tm_n - 1, 8, 128), F32),
            pltpu.VMEM((8, 128), F32),
            dma((12,)), dma((8,)),
            dma((8,)), dma((8,)),
            dma((row_n - 1,)), dma((row_n - 1,)),
            dma((tm_n - 1,)), dma((tm_n - 1,)),
            dma((10,)), dma((10,)),
            dma((4,)), dma((4,)),
            dma((14,)), dma((14,)),
        ],
        compiler_params=pltpu.CompilerParams(collective_id=0, has_side_effects=True, vmem_limit_bytes=58 * MIB),
    )(
        pattern.reshape(8, 4), logit_scale, features, aux, taps, embed_weight, mtok, pos,
        query_weight, key_weight, value_weight,
    )
    return out.reshape(4, 4, 64, 1024)


def solution(mesh):
    slab = ("tm", "row")
    return jax.shard_map(
        functools.partial(per_device, mesh.shape["tm"], mesh.shape["row"]),
        mesh=mesh,
        in_specs=(
            P(*slab, None, None), P(), P(), P(), P(), P(*slab, None), P(), P(), P(*slab, None, None),
            P(), P(), P(), P(), P(*slab, None),
        ),
        out_specs=P(*slab, None, None),
        check_vma=False,
    )
```

```python
import functools

import jax
import jax.numpy as jnp
from jax import lax
from jax.experimental import pallas as pl
from jax.experimental.pallas import tpu as pltpu
from jax.sharding import PartitionSpec as P

MESH = pl.DeviceIdType.MESH
F32, BF16 = jnp.float32, jnp.bfloat16
GROUP = 16
NT_DIMS = (((1,), (1,)), ((), ()))
TN_DIMS = (((0,), (0,)), ((), ()))
MIB = 1 << 20


def remote(src, dst, send, recv, tm, row):
    return pltpu.make_async_remote_copy(
        src_ref=src,
        dst_ref=dst,
        send_sem=send,
        recv_sem=recv,
        device_id={"tm": tm, "row": row},
        device_id_type=MESH,
    )


def group_sum(x):
    lane = lax.broadcasted_iota(jnp.int32, x.shape, 1)
    for k in (1, 2, 4, 8):
        down = pltpu.roll(x, 128 - k, 1)
        up = pltpu.roll(x, k, 1)
        x = x + jnp.where((lane & k) == 0, down, up)
    return x


def mask_rows(mask_token):
    hi = mask_token.astype(BF16).astype(F32)
    mid = (mask_token - hi).astype(BF16).astype(F32)
    low = mask_token - hi - mid
    row = lax.broadcasted_iota(jnp.int32, (16, mask_token.shape[1]), 0)
    zero = jnp.zeros(row.shape, F32)
    return jnp.where(row == 0, hi, jnp.where(row == 1, mid, jnp.where(row == 2, low, zero))).astype(BF16)


def layer_norm(tokens, pos):
    x = tokens + pos.astype(F32)
    c = x - jnp.mean(x, axis=-1, keepdims=True)
    return (c * lax.rsqrt(jnp.mean(c * c, axis=-1, keepdims=True) + 1e-05)).astype(BF16)


def head_norm(y):
    y = y.astype(BF16).astype(F32)
    parts = []
    for i in range(y.shape[1] // 128):
        part = y[:, 128 * i : 128 * (i + 1)]
        parts.append(part * lax.rsqrt(jnp.mean(part * part, axis=-1, keepdims=True) + 1e-06))
    return jnp.concatenate(parts, axis=1).astype(BF16)


def layer(
    tm_n, row_n,
    pattern, scale, feat, aux, taps, embed, mask_token, pos, wq, wk, wv,
    out,
    cells, act, aux_v, taps_v, emb_v, mtok_v, pos_v, w_v, hidden_a, hidden_b, tok, lat_v, q_v, k_v, v_v, out_v,
    mine, stat_r, stat_t, affine,
    load, o_sem, f_send, f_recv, r_send, r_recv, t_send, t_recv, p_send, p_recv, c_send, c_recv, l_send, l_recv,
):
    tm, row = lax.axis_index("tm"), lax.axis_index("row")

    def wrap(i, n):
        return lax.rem(i + n, n)

    before, after = wrap(tm - 1, tm_n), wrap(tm + 1, tm_n)
    above, below = wrap(row - 1, row_n), wrap(row + 1, row_n)

    own = pltpu.make_async_copy(feat, cells.at[1:5, 1:5], load.at[0])
    own.start()
    local = [
        pltpu.make_async_copy(aux, aux_v, load.at[1]),
        pltpu.make_async_copy(taps, taps_v, load.at[2]),
        pltpu.make_async_copy(embed, emb_v.at[0:16], load.at[3]),
        pltpu.make_async_copy(mask_token, mtok_v, load.at[4]),
        *[
            pltpu.make_async_copy(pos.at[2 * t : 2 * t + 2], pos_v.at[4 * t + 5 : 4 * t + 7], load.at[5 + t])
            for t in range(4)
        ],
        pltpu.make_async_copy(wq, w_v.at[0], load.at[9]),
        pltpu.make_async_copy(wk, w_v.at[1], load.at[10]),
        pltpu.make_async_copy(wv, w_v.at[2], load.at[11]),
    ]
    for copy in local:
        copy.start()

    barrier = pltpu.get_barrier_semaphore()
    for d in range(1, row_n):
        pl.semaphore_signal(barrier, inc=1, device_id={"tm": tm, "row": wrap(row + d, row_n)}, device_id_type=MESH)
    for d in range(1, tm_n):
        pl.semaphore_signal(barrier, inc=1, device_id={"tm": wrap(tm + d, tm_n), "row": row}, device_id_type=MESH)
    for t in (before, after):
        for r in (above, below):
            pl.semaphore_signal(barrier, inc=1, device_id={"tm": t, "row": r}, device_id_type=MESH)
    pl.semaphore_wait(barrier, row_n - 1 + tm_n - 1 + 4)

    last, low, high = tm_n - 1, tm_n // 2 - 1, tm_n // 2
    down, up = {}, {}
    for i, t in enumerate((0, 3, 1, 2)):
        down[t] = remote(pos.at[2 * t + 1], pos_v.at[4 * t + 4], p_send.at[i], p_recv.at[i], tm, below)
        up[t] = remote(pos.at[2 * t], pos_v.at[4 * t + 7], p_send.at[4 + i], p_recv.at[4 + i], tm, above)
    at_low, at_high = (tm == low).astype(jnp.int32), (tm == high).astype(jnp.int32)
    to_after = [
        remote(pos.at[6], pos_v.at[1], p_send.at[8], p_recv.at[8], jnp.where(tm == low, 0, after), row),
        remote(
            pos.at[7], pos_v.at[2 + 20 * at_low], p_send.at[9], p_recv.at[9 + 2 * at_low],
            jnp.where(tm == low, last, after), row,
        ),
    ]
    to_before = [
        remote(
            pos.at[0], pos_v.at[21 - 19 * at_high], p_send.at[10], p_recv.at[10 - at_high],
            jnp.where(tm == high, 0, before), row,
        ),
        remote(
            pos.at[1], pos_v.at[22 - at_high], p_send.at[11], p_recv.at[11 - at_high],
            jnp.where(tm == high, last, before), row,
        ),
    ]
    from_first = [
        remote(pos_v.at[1], pos_v.at[1], p_send.at[10], p_recv.at[8], high, row),
        remote(pos_v.at[2], pos_v.at[21], p_send.at[11], p_recv.at[10], low, row),
    ]
    from_last = [
        remote(pos_v.at[22], pos_v.at[2], p_send.at[8], p_recv.at[9], high, row),
        remote(pos_v.at[21], pos_v.at[22], p_send.at[9], p_recv.at[11], low, row),
    ]
    arrive_before = [remote(pos.at[i], pos_v.at[1 + i], p_send.at[8 + i], p_recv.at[8 + i], last - tm, row) for i in range(2)]
    arrive_after = [remote(pos.at[i], pos_v.at[21 + i], p_send.at[10 + i], p_recv.at[10 + i], last - tm, row) for i in range(2)]

    def start_along():
        @pl.when(tm != last)
        def _():
            for copy in to_after:
                copy.start()

        @pl.when(tm != 0)
        def _():
            for copy in to_before:
                copy.start()

    def start_frames(*frames):
        for t in frames:
            down[t].start()
            up[t].start()

    def relay_positions():
        @pl.when(tm == 0)
        def _():
            for copy in arrive_before:
                copy.wait_recv()
            for copy in from_first:
                copy.start()

        @pl.when(tm == last)
        def _():
            for copy in arrive_after:
                copy.wait_recv()
            for copy in from_last:
                copy.start()

    halo = [
        (feat.at[:, 3], cells.at[1:5, 0], tm, below),
        (feat.at[:, 0], cells.at[1:5, 5], tm, above),
        (feat.at[3], cells.at[0, 1:5], after, row),
        (feat.at[0], cells.at[5, 1:5], before, row),
        (feat.at[3, 3], cells.at[0, 0], after, below),
        (feat.at[3, 0], cells.at[0, 5], after, above),
        (feat.at[0, 3], cells.at[5, 0], before, below),
        (feat.at[0, 0], cells.at[5, 5], before, above),
    ]
    feat_copies = [
        remote(src, dst, f_send.at[i], f_recv.at[i], t, r) for i, (src, dst, t, r) in enumerate(halo)
    ]
    for copy in feat_copies:
        copy.start()

    own.wait()
    half = jnp.zeros((8, 512), F32)

    def add_row(i, carry):
        total, square = carry
        x = cells[1 + i // 4, 1 + i % 4].astype(F32)
        for j in range(8):
            part = x[8 * j : 8 * (j + 1)]
            total, square = total + part, square + part * part
        return total, square

    total, square = lax.fori_loop(0, 16, add_row, (half, half))
    total = jnp.sum(total, axis=0, keepdims=True)
    square = jnp.sum(square, axis=0, keepdims=True)
    for i in range(4):
        mine[0, i : i + 1] = total[:, 128 * i : 128 * (i + 1)]
        mine[0, 4 + i : 5 + i] = square[:, 128 * i : 128 * (i + 1)]
    row_copies = [
        remote(mine.at[0], stat_r.at[d - 1], r_send.at[d - 1], r_recv.at[d - 1], tm, wrap(row + d, row_n))
        for d in range(1, row_n)
    ]
    for copy in row_copies:
        copy.start()
    for copy in row_copies:
        copy.wait_recv()
    mine[1] = mine[0] + jnp.sum(stat_r[...], axis=0)
    tm_copies = [
        remote(mine.at[1], stat_t.at[d - 1], t_send.at[d - 1], t_recv.at[d - 1], wrap(tm + d, tm_n), row)
        for d in range(1, tm_n)
    ]
    for copy in tm_copies:
        copy.start()
    start_frames(0)
    for copy in tm_copies:
        copy.wait_recv()

    for copy in local[:5]:
        copy.wait()
    every = group_sum(mine[1] + jnp.sum(stat_t[...], axis=0))
    count = tm_n * row_n * 4 * 4 * 64 * GROUP
    average = every[0:4] / count
    variance = every[4:8] / count - average * average
    inverse = lax.rsqrt(variance + 1e-06)
    affine[0:4] = inverse * aux_v[0:4]
    affine[4:8] = aux_v[4:8] - average * inverse * aux_v[0:4]
    emb_v[16:32] = mask_rows(mtok_v[...])

    for copy in feat_copies:
        copy.wait_recv()

    def activate(i, _):
        f, r = i // 6, i % 6
        frame, line = tm * 4 + f - 1, row * 4 + r - 1
        inside = (frame >= 0) & (frame < tm_n * 4) & (line >= 0) & (line < row_n * 4)
        keep = jnp.where(inside, 0.5, 0.0)
        for j in range(4):
            lanes = slice(128 * j, 128 * (j + 1))
            v = cells[f, r, :, lanes].astype(F32) * affine[j : j + 1] + affine[4 + j : 5 + j]
            v = (v * keep) * (1.0 + jnp.tanh(0.5 * v))
            act[f, pl.ds(pl.multiple_of(r * 64, 64), 64), lanes] = v.astype(BF16)
        return 0

    lax.fori_loop(0, 36, activate, 0)

    column = lax.broadcasted_iota(jnp.int32, (16, 256), 1) % 64
    third = lax.broadcasted_iota(jnp.int32, (16, 128), 0) < 3

    def convolve(t, _):
        acc = jnp.zeros((144, 384), F32)
        for a in range(3):
            acc = acc + lax.dot_general(taps_v[a], act[t + a], NT_DIMS, preferred_element_type=F32)
        sums = []
        for c in range(3):
            part = acc[16 * c : 16 * c + 16]
            for b in (1, 2):
                part = part + pltpu.roll(acc[48 * b + 16 * c : 48 * b + 16 * c + 16], 384 - 64 * b, 1)
            sums.append(part[:, :256])
        left = jnp.where(column == 0, 0.0, pltpu.roll(sums[0], 1, 1))
        right = jnp.where(column == 63, 0.0, pltpu.roll(sums[2], 255, 1))
        out = sums[1] + left + right
        for p in range(2):
            masked = aux_v[pl.ds(24 + 2 * t + p, 1)]
            value = (out[:, 128 * p : 128 * (p + 1)] + aux_v[8:24]).astype(BF16).astype(F32)
            lat_v[4 * t + 5 + p, 0:16] = jnp.where(masked > 0.5, 0.0, value).astype(BF16)
            lat_v[4 * t + 5 + p, 16:32] = jnp.where(third, masked, 0.0).astype(BF16)
        return 0

    lax.fori_loop(0, 4, convolve, 0)

    lat_sends = []
    for t in range(4):
        lat_sends.append((lat_v.at[4 * t + 6], lat_v.at[4 * t + 4], tm, below))
        lat_sends.append((lat_v.at[4 * t + 5], lat_v.at[4 * t + 7], tm, above))
    lat_sends += [
        (lat_v.at[17:19], lat_v.at[1:3], after, row),
        (lat_v.at[5:7], lat_v.at[21:23], before, row),
        (lat_v.at[18], lat_v.at[0], after, below),
        (lat_v.at[17], lat_v.at[3], after, above),
        (lat_v.at[6], lat_v.at[20], before, below),
        (lat_v.at[5], lat_v.at[23], before, above),
    ]
    lat_copies = [remote(src, dst, l_send.at[i], l_recv.at[i], t, r) for i, (src, dst, t, r) in enumerate(lat_sends)]
    for copy in lat_copies:
        copy.start()
    start_along()
    start_frames(3, 1, 2)

    def spot_of(group, i):
        base, a, b = group
        return base + a * (i % 2) + b * (i // 2)

    def normalize(group, i, hidden):
        spot = spot_of(group, i)
        tok[...] = lax.dot_general(lat_v[spot], emb_v[...], TN_DIMS, preferred_element_type=F32)
        for c in range(4):
            rows = slice(32 * c, 32 * c + 32)
            hidden[pl.ds(pl.multiple_of(i * 128 + 32 * c, 32), 32)] = layer_norm(tok[rows], pos_v[spot, rows])

    def project(group, following, hidden, other, own):
        spots = [spot_of(group, j) for j in range(4)]

        def step(i, _):
            columns = pl.ds(pl.multiple_of(i * 256, 256), 256)
            if following is not None:
                normalize(following, i, other)
            if own is not None:
                y = head_norm(jnp.dot(hidden[...], w_v[0, :, columns], preferred_element_type=F32))
                q_v[4 * own : 4 * own + 4, :, columns] = y.reshape(4, 128, 256)
            y = head_norm(jnp.dot(hidden[...], w_v[1, :, columns], preferred_element_type=F32))
            for j in range(4):
                k_v[spots[j], :, columns] = y[128 * j : 128 * (j + 1)]
            y = jnp.dot(hidden[...], w_v[2, :, columns], preferred_element_type=F32).astype(BF16)
            for j in range(4):
                v_v[spots[j], :, columns] = y[128 * j : 128 * (j + 1)]
            return 0

        lax.fori_loop(0, 4, step, 0)

    own_0, own_1, sides = (5, 1, 4), (13, 1, 4), (1, 1, 20)
    ends, corners, middle = (4, 3, 12), (0, 3, 20), (8, 3, 4)
    for copy in local[5:]:
        copy.wait()

    def begin(group):
        def one(i, _):
            normalize(group, i, hidden_a)
            return 0

        lax.fori_loop(0, 4, one, 0)

    begin(own_0)
    project(own_0, own_1, hidden_a, hidden_b, 0)
    project(own_1, None, hidden_b, hidden_a, 1)
    relay_positions()
    for copy in lat_copies:
        copy.wait_recv()

    @pl.when(tm != 0)
    def _():
        for copy in arrive_before:
            copy.wait_recv()

    @pl.when(tm != last)
    def _():
        for copy in arrive_after:
            copy.wait_recv()

    begin(sides)

    odd = lax.rem(row, 2)
    other = row + 1 - 2 * odd
    outer = 3 * odd
    for t in (0, 3):
        down[t].wait_recv()
        up[t].wait_recv()
    outer_before = remote(pos_v.at[4 + outer], pos_v.at[20 + outer], c_send.at[0], c_recv.at[0], before, row)
    outer_after = remote(pos_v.at[16 + outer], pos_v.at[outer], c_send.at[1], c_recv.at[1], after, row)
    inner = [
        remote(pos_v.at[2 - odd], pos_v.at[outer], c_send.at[2], c_recv.at[2], tm, other),
        remote(pos_v.at[22 - odd], pos_v.at[20 + outer], c_send.at[3], c_recv.at[3], tm, other),
    ]
    pl.when(tm != 0)(outer_before.start)
    pl.when(tm != last)(outer_after.start)
    for copy in inner:
        copy.start()
    project(sides, ends, hidden_a, hidden_b, None)
    for t in (1, 2):
        down[t].wait_recv()
        up[t].wait_recv()
    project(ends, middle, hidden_b, hidden_a, None)
    for copy in inner:
        copy.wait_recv()
    pl.when(tm != last)(outer_before.wait_recv)
    pl.when(tm != 0)(outer_after.wait_recv)
    project(middle, corners, hidden_a, hidden_b, None)
    project(corners, None, hidden_b, hidden_a, None)

    def attend(b, _):
        mine_at = 4 * (b // 2) + 5 + b % 2
        spots, live = [], []
        for s in range(4):
            listed = pattern[b, s]
            spot = (listed // (2 * row_n) - tm * 4 + 1) * 4 + listed % (2 * row_n) - row * 2 + 1
            spots.append(jnp.clip(jnp.where(listed >= 0, spot, mine_at), 0, 23))
            live.append(jnp.where(listed >= 0, 1.0, 0.0))

        def heads(g, _):
            columns = [pl.ds(pl.multiple_of(g * 1024 + 128 * u, 128), 128) for u in range(8)]
            scores = []
            for u in range(8):
                keys = jnp.concatenate([k_v[spot, :, columns[u]] for spot in spots], axis=0)
                scores.append(lax.dot_general(q_v[b, :, columns[u]], keys, NT_DIMS, preferred_element_type=F32))
            weights, totals = [], []
            for u in range(8):
                factor = scale[g * 8 + u] / 128.0
                parts = [jnp.exp(scores[u][:, 128 * s : 128 * (s + 1)] * factor) * live[s] for s in range(4)]
                totals.append(jnp.sum((parts[0] + parts[1]) + (parts[2] + parts[3]), axis=-1, keepdims=True))
                weights.append(jnp.concatenate([part.astype(BF16) for part in parts], axis=1))
            for u in range(8):
                values = jnp.concatenate([v_v[spot, :, columns[u]] for spot in spots], axis=0)
                acc = jnp.dot(weights[u], values, preferred_element_type=F32)
                out_v[b, :, columns[u]] = (acc / totals[u]).astype(BF16)
            return 0

        lax.fori_loop(0, 1, heads, 0)
        pltpu.make_async_copy(out_v.at[b], out.at[b], o_sem.at[b]).start()
        return 0

    lax.fori_loop(0, 8, attend, 0)
    for copy in [*feat_copies, *row_copies, *tm_copies, *down.values(), *up.values(), *to_after, *to_before, *lat_copies, *inner]:
        copy.wait_send()
    pl.when(tm != 0)(outer_before.wait_send)
    pl.when(tm != last)(outer_after.wait_send)
    for b in range(8):
        pltpu.make_async_copy(out_v.at[b], out.at[b], o_sem.at[b]).wait()


def per_device(
    tm_n, row_n,
    features, norm_gain, norm_bias, latent_kernel, latent_bias, token_mask, embed_weight, mask_token, pos_embed,
    query_weight, key_weight, value_weight, logit_scale, pattern,
):
    taps = latent_kernel.transpose(1, 2, 3, 0, 4).reshape(3, 144, 512)
    aux = jnp.concatenate(
        [
            norm_gain.reshape(4, 128),
            norm_bias.reshape(4, 128),
            jnp.broadcast_to(latent_bias[:, None], (16, 128)),
            token_mask.reshape(8, 128).astype(F32),
        ]
    )
    pos = pos_embed.reshape(8, 128, 2048)
    mtok = mask_token.reshape(1, 2048)
    anywhere = pl.BlockSpec(memory_space=pl.ANY)
    dma = pltpu.SemaphoreType.DMA
    block = jax.ShapeDtypeStruct((8, 128, 1024), BF16)
    smem = pl.BlockSpec(memory_space=pltpu.SMEM)
    out = pl.pallas_call(
        functools.partial(layer, tm_n, row_n),
        name="layer",
        out_shape=block,
        in_specs=[smem, smem] + [anywhere] * 9,
        out_specs=anywhere,
        scratch_shapes=[
            pltpu.VMEM((6, 6, 64, 512), BF16),
            pltpu.VMEM((6, 384, 512), BF16),
            pltpu.VMEM((32, 128), F32),
            pltpu.VMEM((3, 144, 512), BF16),
            pltpu.VMEM((32, 2048), BF16),
            pltpu.VMEM((1, 2048), F32),
            pltpu.VMEM((24, 128, 2048), BF16),
            pltpu.VMEM((3, 2048, 1024), BF16),
            pltpu.VMEM((512, 2048), BF16),
            pltpu.VMEM((512, 2048), BF16),
            pltpu.VMEM((128, 2048), F32),
            pltpu.VMEM((24, 32, 128), BF16),
            pltpu.VMEM((8, 128, 1024), BF16),
            pltpu.VMEM((24, 128, 1024), BF16),
            pltpu.VMEM((24, 128, 1024), BF16),
            pltpu.VMEM((8, 128, 1024), BF16),
            pltpu.VMEM((2, 8, 128), F32),
            pltpu.VMEM((row_n - 1, 8, 128), F32),
            pltpu.VMEM((tm_n - 1, 8, 128), F32),
            pltpu.VMEM((8, 128), F32),
            dma((12,)), dma((8,)),
            dma((8,)), dma((8,)),
            dma((row_n - 1,)), dma((row_n - 1,)),
            dma((tm_n - 1,)), dma((tm_n - 1,)),
            dma((12,)), dma((12,)),
            dma((4,)), dma((4,)),
            dma((14,)), dma((14,)),
        ],
        compiler_params=pltpu.CompilerParams(collective_id=0, has_side_effects=True, vmem_limit_bytes=58 * MIB),
    )(
        pattern.reshape(8, 4), logit_scale, features, aux, taps, embed_weight, mtok, pos,
        query_weight, key_weight, value_weight,
    )
    return out.reshape(4, 4, 64, 1024)


def solution(mesh):
    slab = ("tm", "row")
    return jax.shard_map(
        functools.partial(per_device, mesh.shape["tm"], mesh.shape["row"]),
        mesh=mesh,
        in_specs=(
            P(*slab, None, None), P(), P(), P(), P(), P(*slab, None), P(), P(), P(*slab, None, None),
            P(), P(), P(), P(), P(*slab, None),
        ),
        out_specs=P(*slab, None, None),
        check_vma=False,
    )
```

```python
import functools

import jax
import jax.numpy as jnp
from jax import lax
from jax.experimental import pallas as pl
from jax.experimental.pallas import tpu as pltpu
from jax.sharding import PartitionSpec as P

MESH = pl.DeviceIdType.MESH
F32, BF16 = jnp.float32, jnp.bfloat16
GROUP = 16
NT_DIMS = (((1,), (1,)), ((), ()))
TN_DIMS = (((0,), (0,)), ((), ()))
MIB = 1 << 20


def remote(src, dst, send, recv, tm, row):
    return pltpu.make_async_remote_copy(
        src_ref=src,
        dst_ref=dst,
        send_sem=send,
        recv_sem=recv,
        device_id={"tm": tm, "row": row},
        device_id_type=MESH,
    )


def group_sum(x):
    lane = lax.broadcasted_iota(jnp.int32, x.shape, 1)
    for k in (1, 2, 4, 8):
        down = pltpu.roll(x, 128 - k, 1)
        up = pltpu.roll(x, k, 1)
        x = x + jnp.where((lane & k) == 0, down, up)
    return x


def mask_rows(mask_token):
    hi = mask_token.astype(BF16).astype(F32)
    mid = (mask_token - hi).astype(BF16).astype(F32)
    low = mask_token - hi - mid
    row = lax.broadcasted_iota(jnp.int32, (16, mask_token.shape[1]), 0)
    zero = jnp.zeros(row.shape, F32)
    return jnp.where(row == 0, hi, jnp.where(row == 1, mid, jnp.where(row == 2, low, zero))).astype(BF16)


def layer_norm(tokens, pos):
    x = tokens + pos.astype(F32)
    c = x - jnp.mean(x, axis=-1, keepdims=True)
    return (c * lax.rsqrt(jnp.mean(c * c, axis=-1, keepdims=True) + 1e-05)).astype(BF16)


def head_norm(y):
    y = y.astype(BF16).astype(F32)
    parts = []
    for i in range(y.shape[1] // 128):
        part = y[:, 128 * i : 128 * (i + 1)]
        parts.append(part * lax.rsqrt(jnp.mean(part * part, axis=-1, keepdims=True) + 1e-06))
    return jnp.concatenate(parts, axis=1).astype(BF16)


def layer(
    tm_n, row_n,
    pattern, scale, feat, aux, taps, embed, mask_token, pos, wq, wk, wv,
    out,
    cells, act, aux_v, taps_v, emb_v, mtok_v, pos_v, w_v, hidden_a, hidden_b, tok, lat_v, q_v, k_v, v_v, out_v,
    mine, stat_r, stat_t, affine,
    load, o_sem, f_send, f_recv, r_send, r_recv, t_send, t_recv, p_send, p_recv, c_send, c_recv, l_send, l_recv,
):
    tm, row = lax.axis_index("tm"), lax.axis_index("row")

    def wrap(i, n):
        return lax.rem(i + n, n)

    before, after = wrap(tm - 1, tm_n), wrap(tm + 1, tm_n)
    above, below = wrap(row - 1, row_n), wrap(row + 1, row_n)

    own = pltpu.make_async_copy(feat, cells.at[1:5, 1:5], load.at[0])
    own.start()
    local = [
        pltpu.make_async_copy(aux, aux_v, load.at[1]),
        pltpu.make_async_copy(taps, taps_v, load.at[2]),
        pltpu.make_async_copy(embed, emb_v.at[0:16], load.at[3]),
        pltpu.make_async_copy(mask_token, mtok_v, load.at[4]),
        *[
            pltpu.make_async_copy(pos.at[2 * t : 2 * t + 2], pos_v.at[4 * t + 5 : 4 * t + 7], load.at[5 + t])
            for t in range(4)
        ],
        pltpu.make_async_copy(wq, w_v.at[0], load.at[9]),
        pltpu.make_async_copy(wk, w_v.at[1], load.at[10]),
        pltpu.make_async_copy(wv, w_v.at[2], load.at[11]),
    ]
    for copy in local:
        copy.start()

    barrier = pltpu.get_barrier_semaphore()
    for d in range(1, row_n):
        pl.semaphore_signal(barrier, inc=1, device_id={"tm": tm, "row": wrap(row + d, row_n)}, device_id_type=MESH)
    for d in range(1, tm_n):
        pl.semaphore_signal(barrier, inc=1, device_id={"tm": wrap(tm + d, tm_n), "row": row}, device_id_type=MESH)
    for t in (before, after):
        for r in (above, below):
            pl.semaphore_signal(barrier, inc=1, device_id={"tm": t, "row": r}, device_id_type=MESH)
    pl.semaphore_wait(barrier, row_n - 1 + tm_n - 1 + 4)

    last, low, high = tm_n - 1, tm_n // 2 - 1, tm_n // 2
    down, up = {}, {}
    for i, t in enumerate((0, 3, 1, 2)):
        down[t] = remote(pos.at[2 * t + 1], pos_v.at[4 * t + 4], p_send.at[i], p_recv.at[i], tm, below)
        up[t] = remote(pos.at[2 * t], pos_v.at[4 * t + 7], p_send.at[4 + i], p_recv.at[4 + i], tm, above)
    at_low, at_high = (tm == low).astype(jnp.int32), (tm == high).astype(jnp.int32)
    to_after = [
        remote(pos.at[6], pos_v.at[1], p_send.at[8], p_recv.at[8], jnp.where(tm == low, 0, after), row),
        remote(
            pos.at[7], pos_v.at[2 + 20 * at_low], p_send.at[9], p_recv.at[9 + 2 * at_low],
            jnp.where(tm == low, last, after), row,
        ),
    ]
    to_before = [
        remote(
            pos.at[0], pos_v.at[21 - 19 * at_high], p_send.at[10], p_recv.at[10 - at_high],
            jnp.where(tm == high, 0, before), row,
        ),
        remote(
            pos.at[1], pos_v.at[22 - at_high], p_send.at[11], p_recv.at[11 - at_high],
            jnp.where(tm == high, last, before), row,
        ),
    ]
    from_first = [
        remote(pos_v.at[1], pos_v.at[1], p_send.at[10], p_recv.at[8], high, row),
        remote(pos_v.at[2], pos_v.at[21], p_send.at[11], p_recv.at[10], low, row),
    ]
    from_last = [
        remote(pos_v.at[22], pos_v.at[2], p_send.at[8], p_recv.at[9], high, row),
        remote(pos_v.at[21], pos_v.at[22], p_send.at[9], p_recv.at[11], low, row),
    ]
    arrive_before = [remote(pos.at[i], pos_v.at[1 + i], p_send.at[8 + i], p_recv.at[8 + i], last - tm, row) for i in range(2)]
    arrive_after = [remote(pos.at[i], pos_v.at[21 + i], p_send.at[10 + i], p_recv.at[10 + i], last - tm, row) for i in range(2)]

    def start_along():
        @pl.when(tm != last)
        def _():
            for copy in to_after:
                copy.start()

        @pl.when(tm != 0)
        def _():
            for copy in to_before:
                copy.start()

    def start_frames(*frames):
        for t in frames:
            down[t].start()
            up[t].start()

    def relay_positions():
        @pl.when(tm == 0)
        def _():
            for copy in arrive_before:
                copy.wait_recv()
            for copy in from_first:
                copy.start()

        @pl.when(tm == last)
        def _():
            for copy in arrive_after:
                copy.wait_recv()
            for copy in from_last:
                copy.start()

    halo = [
        (feat.at[:, 3], cells.at[1:5, 0], tm, below),
        (feat.at[:, 0], cells.at[1:5, 5], tm, above),
        (feat.at[3], cells.at[0, 1:5], after, row),
        (feat.at[0], cells.at[5, 1:5], before, row),
        (feat.at[3, 3], cells.at[0, 0], after, below),
        (feat.at[3, 0], cells.at[0, 5], after, above),
        (feat.at[0, 3], cells.at[5, 0], before, below),
        (feat.at[0, 0], cells.at[5, 5], before, above),
    ]
    feat_copies = [
        remote(src, dst, f_send.at[i], f_recv.at[i], t, r) for i, (src, dst, t, r) in enumerate(halo)
    ]
    for copy in feat_copies:
        copy.start()

    own.wait()
    half = jnp.zeros((8, 512), F32)

    def add_row(i, carry):
        total, square = carry
        x = cells[1 + i // 4, 1 + i % 4].astype(F32)
        for j in range(8):
            part = x[8 * j : 8 * (j + 1)]
            total, square = total + part, square + part * part
        return total, square

    total, square = lax.fori_loop(0, 16, add_row, (half, half))
    total = jnp.sum(total, axis=0, keepdims=True)
    square = jnp.sum(square, axis=0, keepdims=True)
    for i in range(4):
        mine[0, i : i + 1] = total[:, 128 * i : 128 * (i + 1)]
        mine[0, 4 + i : 5 + i] = square[:, 128 * i : 128 * (i + 1)]
    row_copies = [
        remote(mine.at[0], stat_r.at[d - 1], r_send.at[d - 1], r_recv.at[d - 1], tm, wrap(row + d, row_n))
        for d in range(1, row_n)
    ]
    for copy in row_copies:
        copy.start()
    for copy in row_copies:
        copy.wait_recv()
    mine[1] = mine[0] + jnp.sum(stat_r[...], axis=0)
    tm_copies = [
        remote(mine.at[1], stat_t.at[d - 1], t_send.at[d - 1], t_recv.at[d - 1], wrap(tm + d, tm_n), row)
        for d in range(1, tm_n)
    ]
    for copy in tm_copies:
        copy.start()
    start_frames(0)
    for copy in tm_copies:
        copy.wait_recv()

    for copy in local[:5]:
        copy.wait()
    every = group_sum(mine[1] + jnp.sum(stat_t[...], axis=0))
    count = tm_n * row_n * 4 * 4 * 64 * GROUP
    average = every[0:4] / count
    variance = every[4:8] / count - average * average
    inverse = lax.rsqrt(variance + 1e-06)
    affine[0:4] = inverse * aux_v[0:4]
    affine[4:8] = aux_v[4:8] - average * inverse * aux_v[0:4]
    emb_v[16:32] = mask_rows(mtok_v[...])

    for copy in feat_copies:
        copy.wait_recv()

    def activate(i, _):
        f, r = i // 6, i % 6
        frame, line = tm * 4 + f - 1, row * 4 + r - 1
        inside = (frame >= 0) & (frame < tm_n * 4) & (line >= 0) & (line < row_n * 4)
        keep = jnp.where(inside, 0.5, 0.0)
        for j in range(4):
            lanes = slice(128 * j, 128 * (j + 1))
            v = cells[f, r, :, lanes].astype(F32) * affine[j : j + 1] + affine[4 + j : 5 + j]
            v = (v * keep) * (1.0 + jnp.tanh(0.5 * v))
            act[f, pl.ds(pl.multiple_of(r * 64, 64), 64), lanes] = v.astype(BF16)
        return 0

    lax.fori_loop(0, 36, activate, 0)

    column = lax.broadcasted_iota(jnp.int32, (16, 256), 1) % 64
    third = lax.broadcasted_iota(jnp.int32, (16, 128), 0) < 3

    def convolve(t, _):
        acc = jnp.zeros((144, 384), F32)
        for a in range(3):
            acc = acc + lax.dot_general(taps_v[a], act[t + a], NT_DIMS, preferred_element_type=F32)
        sums = []
        for c in range(3):
            part = acc[16 * c : 16 * c + 16]
            for b in (1, 2):
                part = part + pltpu.roll(acc[48 * b + 16 * c : 48 * b + 16 * c + 16], 384 - 64 * b, 1)
            sums.append(part[:, :256])
        left = jnp.where(column == 0, 0.0, pltpu.roll(sums[0], 1, 1))
        right = jnp.where(column == 63, 0.0, pltpu.roll(sums[2], 255, 1))
        out = sums[1] + left + right
        for p in range(2):
            masked = aux_v[pl.ds(24 + 2 * t + p, 1)]
            value = (out[:, 128 * p : 128 * (p + 1)] + aux_v[8:24]).astype(BF16).astype(F32)
            lat_v[4 * t + 5 + p, 0:16] = jnp.where(masked > 0.5, 0.0, value).astype(BF16)
            lat_v[4 * t + 5 + p, 16:32] = jnp.where(third, masked, 0.0).astype(BF16)
        return 0

    lax.fori_loop(0, 4, convolve, 0)

    lat_sends = []
    for t in range(4):
        lat_sends.append((lat_v.at[4 * t + 6], lat_v.at[4 * t + 4], tm, below))
        lat_sends.append((lat_v.at[4 * t + 5], lat_v.at[4 * t + 7], tm, above))
    lat_sends += [
        (lat_v.at[17:19], lat_v.at[1:3], after, row),
        (lat_v.at[5:7], lat_v.at[21:23], before, row),
        (lat_v.at[18], lat_v.at[0], after, below),
        (lat_v.at[17], lat_v.at[3], after, above),
        (lat_v.at[6], lat_v.at[20], before, below),
        (lat_v.at[5], lat_v.at[23], before, above),
    ]
    lat_copies = [remote(src, dst, l_send.at[i], l_recv.at[i], t, r) for i, (src, dst, t, r) in enumerate(lat_sends)]
    for copy in lat_copies:
        copy.start()
    start_along()
    start_frames(3)

    def spot_of(group, i):
        base, a, b = group
        return base + a * (i % 2) + b * (i // 2)

    def normalize(group, i, hidden):
        spot = spot_of(group, i)
        tok[...] = lax.dot_general(lat_v[spot], emb_v[...], TN_DIMS, preferred_element_type=F32)
        for c in range(4):
            rows = slice(32 * c, 32 * c + 32)
            hidden[pl.ds(pl.multiple_of(i * 128 + 32 * c, 32), 32)] = layer_norm(tok[rows], pos_v[spot, rows])

    def project(group, following, hidden, other, own):
        spots = [spot_of(group, j) for j in range(4)]

        def step(i, _):
            columns = pl.ds(pl.multiple_of(i * 256, 256), 256)
            if following is not None:
                normalize(following, i, other)
            if own is not None:
                y = head_norm(jnp.dot(hidden[...], w_v[0, :, columns], preferred_element_type=F32))
                q_v[4 * own : 4 * own + 4, :, columns] = y.reshape(4, 128, 256)
            y = head_norm(jnp.dot(hidden[...], w_v[1, :, columns], preferred_element_type=F32))
            for j in range(4):
                k_v[spots[j], :, columns] = y[128 * j : 128 * (j + 1)]
            y = jnp.dot(hidden[...], w_v[2, :, columns], preferred_element_type=F32).astype(BF16)
            for j in range(4):
                v_v[spots[j], :, columns] = y[128 * j : 128 * (j + 1)]
            return 0

        lax.fori_loop(0, 4, step, 0)

    own_0, own_1, sides = (5, 1, 4), (13, 1, 4), (1, 1, 20)
    ends, corners, middle = (4, 3, 12), (0, 3, 20), (8, 3, 4)
    for copy in local[5:]:
        copy.wait()

    def begin(group):
        def one(i, _):
            normalize(group, i, hidden_a)
            return 0

        lax.fori_loop(0, 4, one, 0)

    begin(own_0)
    project(own_0, own_1, hidden_a, hidden_b, 0)
    start_frames(1, 2)
    project(own_1, None, hidden_b, hidden_a, 1)
    relay_positions()
    for copy in lat_copies:
        copy.wait_recv()
    for t in (0, 3):
        down[t].wait_recv()
        up[t].wait_recv()

    odd = lax.rem(row, 2)
    other = row + 1 - 2 * odd
    outer = 3 * odd
    outer_before = remote(pos_v.at[4 + outer], pos_v.at[20 + outer], c_send.at[0], c_recv.at[0], before, row)
    outer_after = remote(pos_v.at[16 + outer], pos_v.at[outer], c_send.at[1], c_recv.at[1], after, row)
    inner = [
        remote(pos_v.at[2 - odd], pos_v.at[outer], c_send.at[2], c_recv.at[2], tm, other),
        remote(pos_v.at[22 - odd], pos_v.at[20 + outer], c_send.at[3], c_recv.at[3], tm, other),
    ]
    pl.when(tm != 0)(outer_before.start)
    pl.when(tm != last)(outer_after.start)
    begin(ends)
    project(ends, None, hidden_a, hidden_b, None)

    @pl.when(tm != 0)
    def _():
        for copy in arrive_before:
            copy.wait_recv()

    @pl.when(tm != last)
    def _():
        for copy in arrive_after:
            copy.wait_recv()

    for copy in inner:
        copy.start()
    begin(sides)
    for t in (1, 2):
        down[t].wait_recv()
        up[t].wait_recv()
    project(sides, middle, hidden_a, hidden_b, None)
    for copy in inner:
        copy.wait_recv()
    pl.when(tm != last)(outer_before.wait_recv)
    pl.when(tm != 0)(outer_after.wait_recv)
    project(middle, corners, hidden_b, hidden_a, None)
    project(corners, None, hidden_a, hidden_b, None)

    def attend(b, _):
        mine_at = 4 * (b // 2) + 5 + b % 2
        spots, live = [], []
        for s in range(4):
            listed = pattern[b, s]
            spot = (listed // (2 * row_n) - tm * 4 + 1) * 4 + listed % (2 * row_n) - row * 2 + 1
            spots.append(jnp.clip(jnp.where(listed >= 0, spot, mine_at), 0, 23))
            live.append(jnp.where(listed >= 0, 1.0, 0.0))

        def heads(g, _):
            columns = [pl.ds(pl.multiple_of(g * 1024 + 128 * u, 128), 128) for u in range(8)]
            scores = []
            for u in range(8):
                keys = jnp.concatenate([k_v[spot, :, columns[u]] for spot in spots], axis=0)
                scores.append(lax.dot_general(q_v[b, :, columns[u]], keys, NT_DIMS, preferred_element_type=F32))
            weights, totals = [], []
            for u in range(8):
                factor = scale[g * 8 + u] / 128.0
                parts = [jnp.exp(scores[u][:, 128 * s : 128 * (s + 1)] * factor) * live[s] for s in range(4)]
                totals.append(jnp.sum((parts[0] + parts[1]) + (parts[2] + parts[3]), axis=-1, keepdims=True))
                weights.append(jnp.concatenate([part.astype(BF16) for part in parts], axis=1))
            for u in range(8):
                values = jnp.concatenate([v_v[spot, :, columns[u]] for spot in spots], axis=0)
                acc = jnp.dot(weights[u], values, preferred_element_type=F32)
                out_v[b, :, columns[u]] = (acc / totals[u]).astype(BF16)
            return 0

        lax.fori_loop(0, 1, heads, 0)
        pltpu.make_async_copy(out_v.at[b], out.at[b], o_sem.at[b]).start()
        return 0

    lax.fori_loop(0, 8, attend, 0)
    for copy in [*feat_copies, *row_copies, *tm_copies, *down.values(), *up.values(), *to_after, *to_before, *lat_copies, *inner]:
        copy.wait_send()
    pl.when(tm != 0)(outer_before.wait_send)
    pl.when(tm != last)(outer_after.wait_send)
    for b in range(8):
        pltpu.make_async_copy(out_v.at[b], out.at[b], o_sem.at[b]).wait()


def per_device(
    tm_n, row_n,
    features, norm_gain, norm_bias, latent_kernel, latent_bias, token_mask, embed_weight, mask_token, pos_embed,
    query_weight, key_weight, value_weight, logit_scale, pattern,
):
    taps = latent_kernel.transpose(1, 2, 3, 0, 4).reshape(3, 144, 512)
    aux = jnp.concatenate(
        [
            norm_gain.reshape(4, 128),
            norm_bias.reshape(4, 128),
            jnp.broadcast_to(latent_bias[:, None], (16, 128)),
            token_mask.reshape(8, 128).astype(F32),
        ]
    )
    pos = pos_embed.reshape(8, 128, 2048)
    mtok = mask_token.reshape(1, 2048)
    anywhere = pl.BlockSpec(memory_space=pl.ANY)
    dma = pltpu.SemaphoreType.DMA
    block = jax.ShapeDtypeStruct((8, 128, 1024), BF16)
    smem = pl.BlockSpec(memory_space=pltpu.SMEM)
    out = pl.pallas_call(
        functools.partial(layer, tm_n, row_n),
        name="layer",
        out_shape=block,
        in_specs=[smem, smem] + [anywhere] * 9,
        out_specs=anywhere,
        scratch_shapes=[
            pltpu.VMEM((6, 6, 64, 512), BF16),
            pltpu.VMEM((6, 384, 512), BF16),
            pltpu.VMEM((32, 128), F32),
            pltpu.VMEM((3, 144, 512), BF16),
            pltpu.VMEM((32, 2048), BF16),
            pltpu.VMEM((1, 2048), F32),
            pltpu.VMEM((24, 128, 2048), BF16),
            pltpu.VMEM((3, 2048, 1024), BF16),
            pltpu.VMEM((512, 2048), BF16),
            pltpu.VMEM((512, 2048), BF16),
            pltpu.VMEM((128, 2048), F32),
            pltpu.VMEM((24, 32, 128), BF16),
            pltpu.VMEM((8, 128, 1024), BF16),
            pltpu.VMEM((24, 128, 1024), BF16),
            pltpu.VMEM((24, 128, 1024), BF16),
            pltpu.VMEM((8, 128, 1024), BF16),
            pltpu.VMEM((2, 8, 128), F32),
            pltpu.VMEM((row_n - 1, 8, 128), F32),
            pltpu.VMEM((tm_n - 1, 8, 128), F32),
            pltpu.VMEM((8, 128), F32),
            dma((12,)), dma((8,)),
            dma((8,)), dma((8,)),
            dma((row_n - 1,)), dma((row_n - 1,)),
            dma((tm_n - 1,)), dma((tm_n - 1,)),
            dma((12,)), dma((12,)),
            dma((4,)), dma((4,)),
            dma((14,)), dma((14,)),
        ],
        compiler_params=pltpu.CompilerParams(collective_id=0, has_side_effects=True, vmem_limit_bytes=58 * MIB),
    )(
        pattern.reshape(8, 4), logit_scale, features, aux, taps, embed_weight, mtok, pos,
        query_weight, key_weight, value_weight,
    )
    return out.reshape(4, 4, 64, 1024)


def solution(mesh):
    slab = ("tm", "row")
    return jax.shard_map(
        functools.partial(per_device, mesh.shape["tm"], mesh.shape["row"]),
        mesh=mesh,
        in_specs=(
            P(*slab, None, None), P(), P(), P(), P(), P(*slab, None), P(), P(), P(*slab, None, None),
            P(), P(), P(), P(), P(*slab, None),
        ),
        out_specs=P(*slab, None, None),
        check_vma=False,
    )
```

```python
import functools

import jax
import jax.numpy as jnp
from jax import lax
from jax.experimental import pallas as pl
from jax.experimental.pallas import tpu as pltpu
from jax.sharding import PartitionSpec as P

MESH = pl.DeviceIdType.MESH
F32, BF16 = jnp.float32, jnp.bfloat16
GROUP = 16
NT_DIMS = (((1,), (1,)), ((), ()))
TN_DIMS = (((0,), (0,)), ((), ()))
MIB = 1 << 20


def remote(src, dst, send, recv, tm, row):
    return pltpu.make_async_remote_copy(
        src_ref=src,
        dst_ref=dst,
        send_sem=send,
        recv_sem=recv,
        device_id={"tm": tm, "row": row},
        device_id_type=MESH,
    )


def group_sum(x):
    lane = lax.broadcasted_iota(jnp.int32, x.shape, 1)
    for k in (1, 2, 4, 8):
        down = pltpu.roll(x, 128 - k, 1)
        up = pltpu.roll(x, k, 1)
        x = x + jnp.where((lane & k) == 0, down, up)
    return x


def mask_rows(mask_token):
    hi = mask_token.astype(BF16).astype(F32)
    mid = (mask_token - hi).astype(BF16).astype(F32)
    low = mask_token - hi - mid
    row = lax.broadcasted_iota(jnp.int32, (16, mask_token.shape[1]), 0)
    zero = jnp.zeros(row.shape, F32)
    return jnp.where(row == 0, hi, jnp.where(row == 1, mid, jnp.where(row == 2, low, zero))).astype(BF16)


def layer_norm(tokens, pos):
    x = tokens + pos.astype(F32)
    c = x - jnp.mean(x, axis=-1, keepdims=True)
    return (c * lax.rsqrt(jnp.mean(c * c, axis=-1, keepdims=True) + 1e-05)).astype(BF16)


def head_norm(y):
    y = y.astype(BF16).astype(F32)
    parts = []
    for i in range(y.shape[1] // 128):
        part = y[:, 128 * i : 128 * (i + 1)]
        parts.append(part * lax.rsqrt(jnp.mean(part * part, axis=-1, keepdims=True) + 1e-06))
    return jnp.concatenate(parts, axis=1).astype(BF16)


def layer(
    tm_n, row_n,
    pattern, scale, feat, aux, taps, embed, mask_token, pos, wq, wk, wv,
    out,
    cells, act, aux_v, taps_v, emb_v, mtok_v, pos_v, w_v, hidden_a, hidden_b, tok, lat_v, q_v, k_v, v_v, out_v,
    mine, stat_r, stat_t, affine,
    load, o_sem, f_send, f_recv, r_send, r_recv, t_send, t_recv, p_send, p_recv, c_send, c_recv, l_send, l_recv,
):
    tm, row = lax.axis_index("tm"), lax.axis_index("row")

    def wrap(i, n):
        return lax.rem(i + n, n)

    before, after = wrap(tm - 1, tm_n), wrap(tm + 1, tm_n)
    above, below = wrap(row - 1, row_n), wrap(row + 1, row_n)

    own = pltpu.make_async_copy(feat, cells.at[1:5, 1:5], load.at[0])
    own.start()
    local = [
        pltpu.make_async_copy(aux, aux_v, load.at[1]),
        pltpu.make_async_copy(taps, taps_v, load.at[2]),
        pltpu.make_async_copy(embed, emb_v.at[0:16], load.at[3]),
        pltpu.make_async_copy(mask_token, mtok_v, load.at[4]),
        *[
            pltpu.make_async_copy(pos.at[2 * t : 2 * t + 2], pos_v.at[4 * t + 5 : 4 * t + 7], load.at[5 + t])
            for t in range(4)
        ],
        pltpu.make_async_copy(wq, w_v.at[0], load.at[9]),
        pltpu.make_async_copy(wk, w_v.at[1], load.at[10]),
        pltpu.make_async_copy(wv, w_v.at[2], load.at[11]),
    ]
    for copy in local:
        copy.start()

    barrier = pltpu.get_barrier_semaphore()
    for d in range(1, row_n):
        pl.semaphore_signal(barrier, inc=1, device_id={"tm": tm, "row": wrap(row + d, row_n)}, device_id_type=MESH)
    for d in range(1, tm_n):
        pl.semaphore_signal(barrier, inc=1, device_id={"tm": wrap(tm + d, tm_n), "row": row}, device_id_type=MESH)
    for t in (before, after):
        for r in (above, below):
            pl.semaphore_signal(barrier, inc=1, device_id={"tm": t, "row": r}, device_id_type=MESH)
    pl.semaphore_wait(barrier, row_n - 1 + tm_n - 1 + 4)

    last, low, high = tm_n - 1, tm_n // 2 - 1, tm_n // 2
    down, up = {}, {}
    for i, t in enumerate((0, 3, 1, 2)):
        down[t] = remote(pos.at[2 * t + 1], pos_v.at[4 * t + 4], p_send.at[i], p_recv.at[i], tm, below)
        up[t] = remote(pos.at[2 * t], pos_v.at[4 * t + 7], p_send.at[4 + i], p_recv.at[4 + i], tm, above)
    at_low, at_high = (tm == low).astype(jnp.int32), (tm == high).astype(jnp.int32)
    to_after = [
        remote(pos.at[6], pos_v.at[1], p_send.at[8], p_recv.at[8], jnp.where(tm == low, 0, after), row),
        remote(
            pos.at[7], pos_v.at[2 + 20 * at_low], p_send.at[9], p_recv.at[9 + 2 * at_low],
            jnp.where(tm == low, last, after), row,
        ),
    ]
    to_before = [
        remote(
            pos.at[0], pos_v.at[21 - 19 * at_high], p_send.at[10], p_recv.at[10 - at_high],
            jnp.where(tm == high, 0, before), row,
        ),
        remote(
            pos.at[1], pos_v.at[22 - at_high], p_send.at[11], p_recv.at[11 - at_high],
            jnp.where(tm == high, last, before), row,
        ),
    ]
    from_first = [
        remote(pos_v.at[1], pos_v.at[1], p_send.at[10], p_recv.at[8], high, row),
        remote(pos_v.at[2], pos_v.at[21], p_send.at[11], p_recv.at[10], low, row),
    ]
    from_last = [
        remote(pos_v.at[22], pos_v.at[2], p_send.at[8], p_recv.at[9], high, row),
        remote(pos_v.at[21], pos_v.at[22], p_send.at[9], p_recv.at[11], low, row),
    ]
    arrive_before = [remote(pos.at[i], pos_v.at[1 + i], p_send.at[8 + i], p_recv.at[8 + i], last - tm, row) for i in range(2)]
    arrive_after = [remote(pos.at[i], pos_v.at[21 + i], p_send.at[10 + i], p_recv.at[10 + i], last - tm, row) for i in range(2)]

    def start_along():
        @pl.when(tm != last)
        def _():
            for copy in to_after:
                copy.start()

        @pl.when(tm != 0)
        def _():
            for copy in to_before:
                copy.start()

    def start_frames(*frames):
        for t in frames:
            down[t].start()
            up[t].start()

    def relay_positions():
        @pl.when(tm == 0)
        def _():
            for copy in arrive_before:
                copy.wait_recv()
            for copy in from_first:
                copy.start()

        @pl.when(tm == last)
        def _():
            for copy in arrive_after:
                copy.wait_recv()
            for copy in from_last:
                copy.start()

    halo = [
        (feat.at[:, 3], cells.at[1:5, 0], tm, below),
        (feat.at[:, 0], cells.at[1:5, 5], tm, above),
        (feat.at[3], cells.at[0, 1:5], after, row),
        (feat.at[0], cells.at[5, 1:5], before, row),
        (feat.at[3, 3], cells.at[0, 0], after, below),
        (feat.at[3, 0], cells.at[0, 5], after, above),
        (feat.at[0, 3], cells.at[5, 0], before, below),
        (feat.at[0, 0], cells.at[5, 5], before, above),
    ]
    feat_copies = [
        remote(src, dst, f_send.at[i], f_recv.at[i], t, r) for i, (src, dst, t, r) in enumerate(halo)
    ]
    for copy in feat_copies:
        copy.start()

    own.wait()
    half = jnp.zeros((8, 512), F32)

    def add_row(i, carry):
        total, square = carry
        x = cells[1 + i // 4, 1 + i % 4].astype(F32)
        for j in range(8):
            part = x[8 * j : 8 * (j + 1)]
            total, square = total + part, square + part * part
        return total, square

    total, square = lax.fori_loop(0, 16, add_row, (half, half), unroll=2)
    total = jnp.sum(total, axis=0, keepdims=True)
    square = jnp.sum(square, axis=0, keepdims=True)
    for i in range(4):
        mine[0, i : i + 1] = total[:, 128 * i : 128 * (i + 1)]
        mine[0, 4 + i : 5 + i] = square[:, 128 * i : 128 * (i + 1)]
    row_copies = [
        remote(mine.at[0], stat_r.at[d - 1], r_send.at[d - 1], r_recv.at[d - 1], tm, wrap(row + d, row_n))
        for d in range(1, row_n)
    ]
    for copy in row_copies:
        copy.start()
    for copy in row_copies:
        copy.wait_recv()
    mine[1] = mine[0] + jnp.sum(stat_r[...], axis=0)
    tm_copies = [
        remote(mine.at[1], stat_t.at[d - 1], t_send.at[d - 1], t_recv.at[d - 1], wrap(tm + d, tm_n), row)
        for d in range(1, tm_n)
    ]
    for copy in tm_copies:
        copy.start()
    start_frames(0)
    for copy in tm_copies:
        copy.wait_recv()

    for copy in local[:5]:
        copy.wait()
    every = group_sum(mine[1] + jnp.sum(stat_t[...], axis=0))
    count = tm_n * row_n * 4 * 4 * 64 * GROUP
    average = every[0:4] / count
    variance = every[4:8] / count - average * average
    inverse = lax.rsqrt(variance + 1e-06)
    affine[0:4] = inverse * aux_v[0:4]
    affine[4:8] = aux_v[4:8] - average * inverse * aux_v[0:4]
    emb_v[16:32] = mask_rows(mtok_v[...])

    for copy in feat_copies:
        copy.wait_recv()

    def activate(i, _):
        f, r = i // 6, i % 6
        frame, line = tm * 4 + f - 1, row * 4 + r - 1
        inside = (frame >= 0) & (frame < tm_n * 4) & (line >= 0) & (line < row_n * 4)
        keep = jnp.where(inside, 0.5, 0.0)
        for j in range(4):
            lanes = slice(128 * j, 128 * (j + 1))
            v = cells[f, r, :, lanes].astype(F32) * affine[j : j + 1] + affine[4 + j : 5 + j]
            v = (v * keep) * (1.0 + jnp.tanh(0.5 * v))
            act[f, pl.ds(pl.multiple_of(r * 64, 64), 64), lanes] = v.astype(BF16)
        return 0

    lax.fori_loop(0, 36, activate, 0, unroll=2)

    column = lax.broadcasted_iota(jnp.int32, (16, 256), 1) % 64
    third = lax.broadcasted_iota(jnp.int32, (16, 128), 0) < 3

    def convolve(t, _):
        acc = jnp.zeros((144, 384), F32)
        for a in range(3):
            acc = acc + lax.dot_general(taps_v[a], act[t + a], NT_DIMS, preferred_element_type=F32)
        sums = []
        for c in range(3):
            part = acc[16 * c : 16 * c + 16]
            for b in (1, 2):
                part = part + pltpu.roll(acc[48 * b + 16 * c : 48 * b + 16 * c + 16], 384 - 64 * b, 1)
            sums.append(part[:, :256])
        left = jnp.where(column == 0, 0.0, pltpu.roll(sums[0], 1, 1))
        right = jnp.where(column == 63, 0.0, pltpu.roll(sums[2], 255, 1))
        out = sums[1] + left + right
        for p in range(2):
            masked = aux_v[pl.ds(24 + 2 * t + p, 1)]
            value = (out[:, 128 * p : 128 * (p + 1)] + aux_v[8:24]).astype(BF16).astype(F32)
            lat_v[4 * t + 5 + p, 0:16] = jnp.where(masked > 0.5, 0.0, value).astype(BF16)
            lat_v[4 * t + 5 + p, 16:32] = jnp.where(third, masked, 0.0).astype(BF16)
        return 0

    lax.fori_loop(0, 4, convolve, 0, unroll=2)

    lat_sends = []
    for t in range(4):
        lat_sends.append((lat_v.at[4 * t + 6], lat_v.at[4 * t + 4], tm, below))
        lat_sends.append((lat_v.at[4 * t + 5], lat_v.at[4 * t + 7], tm, above))
    lat_sends += [
        (lat_v.at[17:19], lat_v.at[1:3], after, row),
        (lat_v.at[5:7], lat_v.at[21:23], before, row),
        (lat_v.at[18], lat_v.at[0], after, below),
        (lat_v.at[17], lat_v.at[3], after, above),
        (lat_v.at[6], lat_v.at[20], before, below),
        (lat_v.at[5], lat_v.at[23], before, above),
    ]
    lat_copies = [remote(src, dst, l_send.at[i], l_recv.at[i], t, r) for i, (src, dst, t, r) in enumerate(lat_sends)]
    for copy in lat_copies:
        copy.start()
    start_along()
    start_frames(3)

    def spot_of(group, i):
        base, a, b = group
        return base + a * (i % 2) + b * (i // 2)

    def normalize(group, i, hidden):
        spot = spot_of(group, i)
        tok[...] = lax.dot_general(lat_v[spot], emb_v[...], TN_DIMS, preferred_element_type=F32)
        for c in range(4):
            rows = slice(32 * c, 32 * c + 32)
            hidden[pl.ds(pl.multiple_of(i * 128 + 32 * c, 32), 32)] = layer_norm(tok[rows], pos_v[spot, rows])

    def project(group, following, hidden, other, own):
        spots = [spot_of(group, j) for j in range(4)]

        def step(i, _):
            columns = pl.ds(pl.multiple_of(i * 256, 256), 256)
            if following is not None:
                normalize(following, i, other)
            if own is not None:
                y = head_norm(jnp.dot(hidden[...], w_v[0, :, columns], preferred_element_type=F32))
                q_v[4 * own : 4 * own + 4, :, columns] = y.reshape(4, 128, 256)
            y = head_norm(jnp.dot(hidden[...], w_v[1, :, columns], preferred_element_type=F32))
            for j in range(4):
                k_v[spots[j], :, columns] = y[128 * j : 128 * (j + 1)]
            y = jnp.dot(hidden[...], w_v[2, :, columns], preferred_element_type=F32).astype(BF16)
            for j in range(4):
                v_v[spots[j], :, columns] = y[128 * j : 128 * (j + 1)]
            return 0

        lax.fori_loop(0, 4, step, 0)

    own_0, own_1, sides = (5, 1, 4), (13, 1, 4), (1, 1, 20)
    ends, corners, middle = (4, 3, 12), (0, 3, 20), (8, 3, 4)
    for copy in local[5:]:
        copy.wait()

    def begin(group):
        def one(i, _):
            normalize(group, i, hidden_a)
            return 0

        lax.fori_loop(0, 4, one, 0)

    begin(own_0)
    project(own_0, own_1, hidden_a, hidden_b, 0)
    start_frames(1, 2)
    project(own_1, None, hidden_b, hidden_a, 1)
    relay_positions()
    for copy in lat_copies:
        copy.wait_recv()
    for t in (0, 3):
        down[t].wait_recv()
        up[t].wait_recv()

    odd = lax.rem(row, 2)
    other = row + 1 - 2 * odd
    outer = 3 * odd
    outer_before = remote(pos_v.at[4 + outer], pos_v.at[20 + outer], c_send.at[0], c_recv.at[0], before, row)
    outer_after = remote(pos_v.at[16 + outer], pos_v.at[outer], c_send.at[1], c_recv.at[1], after, row)
    inner = [
        remote(pos_v.at[2 - odd], pos_v.at[outer], c_send.at[2], c_recv.at[2], tm, other),
        remote(pos_v.at[22 - odd], pos_v.at[20 + outer], c_send.at[3], c_recv.at[3], tm, other),
    ]
    pl.when(tm != 0)(outer_before.start)
    pl.when(tm != last)(outer_after.start)
    begin(ends)
    project(ends, None, hidden_a, hidden_b, None)

    @pl.when(tm != 0)
    def _():
        for copy in arrive_before:
            copy.wait_recv()

    @pl.when(tm != last)
    def _():
        for copy in arrive_after:
            copy.wait_recv()

    for copy in inner:
        copy.start()
    begin(sides)
    for t in (1, 2):
        down[t].wait_recv()
        up[t].wait_recv()
    project(sides, middle, hidden_a, hidden_b, None)
    for copy in inner:
        copy.wait_recv()
    pl.when(tm != last)(outer_before.wait_recv)
    pl.when(tm != 0)(outer_after.wait_recv)
    project(middle, corners, hidden_b, hidden_a, None)
    project(corners, None, hidden_a, hidden_b, None)

    def attend(b, _):
        mine_at = 4 * (b // 2) + 5 + b % 2
        spots, live = [], []
        for s in range(4):
            listed = pattern[b, s]
            spot = (listed // (2 * row_n) - tm * 4 + 1) * 4 + listed % (2 * row_n) - row * 2 + 1
            spots.append(jnp.clip(jnp.where(listed >= 0, spot, mine_at), 0, 23))
            live.append(jnp.where(listed >= 0, 1.0, 0.0))

        def heads(g, _):
            columns = [pl.ds(pl.multiple_of(g * 1024 + 128 * u, 128), 128) for u in range(8)]
            scores = []
            for u in range(8):
                keys = jnp.concatenate([k_v[spot, :, columns[u]] for spot in spots], axis=0)
                scores.append(lax.dot_general(q_v[b, :, columns[u]], keys, NT_DIMS, preferred_element_type=F32))
            weights, totals = [], []
            for u in range(8):
                factor = scale[g * 8 + u] / 128.0
                parts = [jnp.exp(scores[u][:, 128 * s : 128 * (s + 1)] * factor) * live[s] for s in range(4)]
                totals.append(jnp.sum((parts[0] + parts[1]) + (parts[2] + parts[3]), axis=-1, keepdims=True))
                weights.append(jnp.concatenate([part.astype(BF16) for part in parts], axis=1))
            for u in range(8):
                values = jnp.concatenate([v_v[spot, :, columns[u]] for spot in spots], axis=0)
                acc = jnp.dot(weights[u], values, preferred_element_type=F32)
                out_v[b, :, columns[u]] = (acc / totals[u]).astype(BF16)
            return 0

        lax.fori_loop(0, 1, heads, 0)
        pltpu.make_async_copy(out_v.at[b], out.at[b], o_sem.at[b]).start()
        return 0

    lax.fori_loop(0, 8, attend, 0)
    for copy in [*feat_copies, *row_copies, *tm_copies, *down.values(), *up.values(), *to_after, *to_before, *lat_copies, *inner]:
        copy.wait_send()
    pl.when(tm != 0)(outer_before.wait_send)
    pl.when(tm != last)(outer_after.wait_send)
    for b in range(8):
        pltpu.make_async_copy(out_v.at[b], out.at[b], o_sem.at[b]).wait()


def per_device(
    tm_n, row_n,
    features, norm_gain, norm_bias, latent_kernel, latent_bias, token_mask, embed_weight, mask_token, pos_embed,
    query_weight, key_weight, value_weight, logit_scale, pattern,
):
    taps = latent_kernel.transpose(1, 2, 3, 0, 4).reshape(3, 144, 512)
    aux = jnp.concatenate(
        [
            norm_gain.reshape(4, 128),
            norm_bias.reshape(4, 128),
            jnp.broadcast_to(latent_bias[:, None], (16, 128)),
            token_mask.reshape(8, 128).astype(F32),
        ]
    )
    pos = pos_embed.reshape(8, 128, 2048)
    mtok = mask_token.reshape(1, 2048)
    anywhere = pl.BlockSpec(memory_space=pl.ANY)
    dma = pltpu.SemaphoreType.DMA
    block = jax.ShapeDtypeStruct((8, 128, 1024), BF16)
    smem = pl.BlockSpec(memory_space=pltpu.SMEM)
    out = pl.pallas_call(
        functools.partial(layer, tm_n, row_n),
        name="layer",
        out_shape=block,
        in_specs=[smem, smem] + [anywhere] * 9,
        out_specs=anywhere,
        scratch_shapes=[
            pltpu.VMEM((6, 6, 64, 512), BF16),
            pltpu.VMEM((6, 384, 512), BF16),
            pltpu.VMEM((32, 128), F32),
            pltpu.VMEM((3, 144, 512), BF16),
            pltpu.VMEM((32, 2048), BF16),
            pltpu.VMEM((1, 2048), F32),
            pltpu.VMEM((24, 128, 2048), BF16),
            pltpu.VMEM((3, 2048, 1024), BF16),
            pltpu.VMEM((512, 2048), BF16),
            pltpu.VMEM((512, 2048), BF16),
            pltpu.VMEM((128, 2048), F32),
            pltpu.VMEM((24, 32, 128), BF16),
            pltpu.VMEM((8, 128, 1024), BF16),
            pltpu.VMEM((24, 128, 1024), BF16),
            pltpu.VMEM((24, 128, 1024), BF16),
            pltpu.VMEM((8, 128, 1024), BF16),
            pltpu.VMEM((2, 8, 128), F32),
            pltpu.VMEM((row_n - 1, 8, 128), F32),
            pltpu.VMEM((tm_n - 1, 8, 128), F32),
            pltpu.VMEM((8, 128), F32),
            dma((12,)), dma((8,)),
            dma((8,)), dma((8,)),
            dma((row_n - 1,)), dma((row_n - 1,)),
            dma((tm_n - 1,)), dma((tm_n - 1,)),
            dma((12,)), dma((12,)),
            dma((4,)), dma((4,)),
            dma((14,)), dma((14,)),
        ],
        compiler_params=pltpu.CompilerParams(collective_id=0, has_side_effects=True, vmem_limit_bytes=58 * MIB),
    )(
        pattern.reshape(8, 4), logit_scale, features, aux, taps, embed_weight, mtok, pos,
        query_weight, key_weight, value_weight,
    )
    return out.reshape(4, 4, 64, 1024)


def solution(mesh):
    slab = ("tm", "row")
    return jax.shard_map(
        functools.partial(per_device, mesh.shape["tm"], mesh.shape["row"]),
        mesh=mesh,
        in_specs=(
            P(*slab, None, None), P(), P(), P(), P(), P(*slab, None), P(), P(), P(*slab, None, None),
            P(), P(), P(), P(), P(*slab, None),
        ),
        out_specs=P(*slab, None, None),
        check_vma=False,
    )
```
